512 devices in a mesh: row: 32 (over x_lo, y, core), col: 16 (over z, x_hi).
Axes of the slice: x: 4 (x_hi: 2, x_lo: 2; x = x_hi * 2 + x_lo), y: 8, z: 8, core: 2. Of those that a mesh axis runs over, the one named last changes fastest.
Arguments:
- counts: int32 [131072, 4096], P(('row', 'col')), may hold values from 0 to 1024, as said below
- row_marg: int32 [131072], P(('row', 'col')), may hold values from 64 to 999999
- col_marg: int32 [4096], P('col'), may hold values from 64 to 999999
- log_total: float32 [1], replicated, may hold values from 22 to 26
- row_embed: float32 [131072, 256], P(('row', 'col')), may hold values from -0.6 to 0.6
- col_embed: float32 [4096, 256], P('col'), may hold values from -0.6 to 0.6
Outputs:
- row_grad: float32 [131072, 256], P(('row', 'col'))
- col_grad: float32 [4096, 256], P('col')
The draws below stay inside these ranges and needn't reach their ends.
Inputs may be any that keep to these rules, and one draw needn't show every extreme that they name: About a quarter of the counts are zero; the positive ones spread over powers of two.
All inputs are finite; a program needn't handle non-finite values.
Results may differ from the reference program's by a relative error of at most 0.0003.
Values sent between devices are 32-bit elements; how exact they have to be, the bound alone decides.
No kernel may reach another device: no remote copies, remote signals or barrier semaphores. Data moves between devices by JAX's collectives and lax.ppermute only.
A program may use at most 64 MiB of HBM per device.

```python
import math
import jax
import jax.numpy as jnp
from jax import lax

D = 256
ROWS = 131072
COLS = 4096
N_ROW = 32


def draw_counts(key, part):
    key_one, key_two, key_three = jax.random.split(key, 3)
    present = jax.random.randint(key_one, (ROWS, COLS), 0, 4) > 0
    expon = jax.random.randint(key_two, (ROWS, COLS), 0, 11)
    upper = jnp.power(2, expon).astype(jnp.int32) + 1
    values = jax.random.randint(key_three, (ROWS, COLS), 1, upper)
    return jnp.where(present, values, 0).astype(jnp.int32)


def set_ends(entries, rng, least, largest):
    extent = entries.shape
    place = [jax.random.randint(jax.random.fold_in(rng, axis), (), 0, extent[axis]) for axis in range(len(extent))]
    entries = entries.at[tuple(place)].set(least)
    longest = extent.index(max(extent))
    place[longest] = (place[longest] + 1) % extent[longest]
    return entries.at[tuple(place)].set(largest)


def level_of(stream_key, extent, cuts, low, largest):
    level = 1.0
    for dim, parts in cuts:
        heights = jax.random.uniform(jax.random.fold_in(jax.random.fold_in(stream_key, 6), dim), (parts,), jnp.float32, low / len(cuts), largest / len(cuts))
        level = level * jnp.repeat(jnp.exp(heights), extent[dim] // parts).reshape((-1,) + (1,) * (len(extent) - 1 - dim))
    return level


def normal_values(stream_key, extent, deviation, reach, shards=(), kind=jnp.bfloat16):
    drawn = jax.random.normal(stream_key, extent, jnp.float32) * deviation
    if len(shards) > 0:
        drawn = level_of(stream_key, extent, shards, -0.22, 0.18) * drawn
    return jnp.clip(drawn, min=-reach, max=reach).astype(kind)


def setup_inputs(seed: int = 0) -> dict:
    key_of = jax.random.split(jax.random.key(seed), 7)
    counts = draw_counts(jax.random.fold_in(key_of[6], 71), 0)
    row_marg = set_ends(jax.random.randint(key_of[1], (ROWS,), 64, 1000000), jax.random.fold_in(key_of[1], 1), 64, 999999).astype(jnp.int32)
    col_marg = set_ends(jax.random.randint(key_of[2], (COLS,), 64, 1000000), jax.random.fold_in(key_of[2], 1), 64, 999999).astype(jnp.int32)
    log_total = jnp.clip(jax.random.uniform(key_of[3], (1,), jnp.float32, 22.0, 26.0), 22.0, 26.0)
    row_embed = normal_values(key_of[4], (ROWS, D), 0.1, 0.6, ((0, 512),), jnp.float32)
    col_embed = normal_values(key_of[5], (COLS, D), 0.1, 0.6, ((0, 16),), jnp.float32)
    return {"counts": counts, "row_marg": row_marg, "col_marg": col_marg, "log_total": log_total, "row_embed": row_embed, "col_embed": col_embed}


def cell_grads(cnt, score, base):
    x = cnt.astype(jnp.float32)
    pmi = jnp.log(jnp.maximum(x, 1.0)) + base
    weight = 0.1 + 0.25 * jnp.sqrt(x)
    return jnp.where(cnt > 0, weight * (score - pmi), jax.nn.sigmoid(score - base))

def reference(counts, row_marg, col_marg, log_total, row_embed, col_embed):
    log_col = jnp.log(col_marg.astype(jnp.float32))
    blocks = N_ROW
    block_rows = ROWS // blocks

    def step(acc, index):
        start = index * block_rows
        wblock = lax.dynamic_slice_in_dim(row_embed, start, block_rows, 0)
        cblock = lax.dynamic_slice_in_dim(counts, start, block_rows, 0)
        mblock = lax.dynamic_slice_in_dim(row_marg, start, block_rows, 0)
        score = jnp.dot(wblock, col_embed.T, precision=lax.Precision.HIGHEST, preferred_element_type=jnp.float32)
        base = log_total[0] - jnp.log(mblock.astype(jnp.float32))[:, None] - log_col[None, :]
        cell = cell_grads(cblock, score, base)
        rgrad = jnp.dot(cell, col_embed, precision=lax.Precision.HIGHEST, preferred_element_type=jnp.float32)
        acc = acc + jnp.dot(cell.T, wblock, precision=lax.Precision.HIGHEST, preferred_element_type=jnp.float32)
        return (acc, rgrad)
    acc, rgrads = lax.scan(step, jnp.zeros((COLS, D), jnp.float32), jnp.arange(blocks, dtype=jnp.int32))
    row_grad = rgrads.reshape(ROWS, D) / math.sqrt(COLS)
    col_grad = acc / math.sqrt(ROWS)
    return (row_grad, col_grad)
```

```python
import functools
import math

import jax
import jax.numpy as jnp
import numpy as np
from jax import lax
from jax.experimental import pallas as pl
from jax.experimental.pallas import tpu as pltpu
from jax.sharding import Mesh, PartitionSpec as P

AXES = ("xlo", "y", "core", "z", "xhi")
SIZES = (2, 8, 2, 8, 2)
DIM = 256
ROWS = 256
SLICE = 64
PACK = 72


def pairs_to(move):
    pairs = []
    for target in range(math.prod(SIZES)):
        at = dict(zip(AXES, (int(i) for i in np.unravel_index(target, SIZES))))
        at.update(move(at))
        pairs.append((int(np.ravel_multi_index([at[a] for a in AXES], SIZES)), target))
    return pairs


def core_swap(at):
    return {"core": 1 - at["core"]}


def x_pair(at):
    return {"xlo": 1 - at["xlo"]}


def x_next(at):
    return {"xlo": 1 - at["xlo"], "xhi": 1 - at["xhi"]}


def x_far(at):
    return {"xhi": 1 - at["xhi"]}


def fetch(value, move):
    return lax.ppermute(value, AXES, pairs_to(move))


def split(value):
    high = value.astype(jnp.bfloat16)
    return high, (value - high.astype(jnp.float32)).astype(jnp.bfloat16)


def dot3(a, b, dims):
    one = functools.partial(
        lax.dot_general, dimension_numbers=(dims, ((), ())), preferred_element_type=jnp.float32
    )
    return one(a[0], b[0]) + (one(a[0], b[1]) + one(a[1], b[0]))


def cells_kernel(
    where, c_own_a, c_own_b, c_oth_a, c_oth_b, rb_own, rb_oth, s_own, s_pair, s_next, s_far,
    r_own, r_oth, g_own, g_pair, g_next, g_far,
    rh, rl, th, tl, emb, logs, gs,
):
    step = pl.program_id(0)

    @pl.when(step == 0)
    def _():
        for k, ref in enumerate((rb_own, rb_oth)):
            high, low = split(ref[:, :DIM])
            rh[k * ROWS : (k + 1) * ROWS, :] = high
            rl[k * ROWS : (k + 1) * ROWS, :] = low
            high, low = split(ref[:, :DIM].T)
            th[:, k * ROWS : (k + 1) * ROWS] = high
            tl[:, k * ROWS : (k + 1) * ROWS] = low
        r_own[...] = jnp.zeros_like(r_own)
        r_oth[...] = jnp.zeros_like(r_oth)

    off = pl.multiple_of(where[2] * SLICE, SLICE)
    rest = pl.multiple_of((1 - where[2]) * SLICE, SLICE)
    emb[pl.ds(off, SLICE), :] = s_own[0, :SLICE, :]
    emb[pl.ds(rest, SLICE), :] = s_pair[0, :SLICE, :]
    emb[pl.ds(2 * SLICE + off, SLICE), :] = s_far[0, :SLICE, :]
    emb[pl.ds(2 * SLICE + rest, SLICE), :] = s_next[0, :SLICE, :]
    logs[:, :128] = s_own[0, SLICE:, :128] + s_pair[0, SLICE:, :128]
    logs[:, 128:] = s_far[0, SLICE:, :128] + s_next[0, SLICE:, :128]
    e = split(emb[...])
    log_col = logs[0:1, :]
    total = None
    for k, (c_a, c_b, rb, r_out) in enumerate(
        ((c_own_a, c_own_b, rb_own, r_own), (c_oth_a, c_oth_b, rb_oth, r_oth))
    ):
        part = slice(k * ROWS, (k + 1) * ROWS)
        score = dot3((rh[part, :], rl[part, :]), e, ((1,), (1,)))
        gap = score - rb[:, DIM : DIM + 1] + log_col
        cnt = jnp.concatenate([c_a[...], c_b[...]], axis=1)
        x = cnt.astype(jnp.float32)
        weight = 0.1 + 0.25 * jnp.sqrt(x)
        cell = jnp.where(
            cnt > 0,
            weight * (gap - jnp.log(jnp.maximum(x, 1.0))),
            1.0 / (1.0 + jnp.exp(-gap)),
        )
        cell = split(cell)
        r_out[...] += dot3(cell, e, ((1,), (0,)))
        term = dot3((th[:, part], tl[:, part]), cell, ((1,), (0,)))
        total = term if total is None else total + term
    gs[...] = total.T
    g_own[0] = gs[pl.ds(off, SLICE), :]
    g_pair[0] = gs[pl.ds(rest, SLICE), :]
    g_far[0] = gs[pl.ds(2 * SLICE + off, SLICE), :]
    g_next[0] = gs[pl.ds(2 * SLICE + rest, SLICE), :]


def cells(where, counts, counts_oth, rb, rb_oth, slices):
    def block(same):
        def at(z, w):
            xhi = w[1] if same else 1 - w[1]
            return (0, z * 4 + xhi * 2 + w[0])

        return pl.BlockSpec((ROWS, 128), at)

    whole = pl.BlockSpec((ROWS, DIM + 128), lambda z, w: (0, 0))
    pack = pl.BlockSpec((1, PACK, DIM), lambda z, w: (z, 0, 0))
    r_out = pl.BlockSpec((ROWS, DIM), lambda z, w: (0, 0))
    g_out = pl.BlockSpec((1, SLICE, DIM), lambda z, w: (z, 0, 0))
    f32 = jnp.float32
    return pl.pallas_call(
        cells_kernel,
        grid_spec=pltpu.PrefetchScalarGridSpec(
            num_scalar_prefetch=1,
            grid=(8,),
            in_specs=[block(True), block(False), block(True), block(False), whole, whole] + [pack] * 4,
            out_specs=[r_out] * 2 + [g_out] * 4,
            scratch_shapes=[
                pltpu.VMEM((2 * ROWS, DIM), jnp.bfloat16),
                pltpu.VMEM((2 * ROWS, DIM), jnp.bfloat16),
                pltpu.VMEM((DIM, 2 * ROWS), jnp.bfloat16),
                pltpu.VMEM((DIM, 2 * ROWS), jnp.bfloat16),
                pltpu.VMEM((4 * SLICE, DIM), f32),
                pltpu.VMEM((PACK - SLICE, DIM), f32),
                pltpu.VMEM((4 * SLICE, DIM), f32),
            ],
        ),
        out_shape=[jax.ShapeDtypeStruct((ROWS, DIM), f32)] * 2
        + [jax.ShapeDtypeStruct((8, SLICE, DIM), f32)] * 4,
        compiler_params=pltpu.CompilerParams(vmem_limit_bytes=40 * 2**20),
        cost_estimate=pl.CostEstimate(
            flops=3 * 3 * 2 * 512 * 2048 * 256, bytes_accessed=10 * 2**20, transcendentals=4 * 2**20
        ),
    )(where, counts, counts, counts_oth, counts_oth, rb, rb_oth, *slices)


def body(counts, row_marg, col_marg, log_total, row_embed, col_embed):
    core, xlo, xhi = (lax.axis_index(a) for a in ("core", "xlo", "xhi"))
    where = jnp.stack([core, xhi, xlo]).astype(jnp.int32)

    counts_oth = fetch(counts, core_swap)
    base_row = log_total[0] - jnp.log(row_marg.astype(jnp.float32))
    rb = jnp.concatenate([row_embed, jnp.broadcast_to(base_row[:, None], (ROWS, 128))], axis=1)
    rb_oth = fetch(rb, core_swap)

    start = (core * 2 + xlo) * SLICE
    embeds = lax.dynamic_slice_in_dim(col_embed, start, SLICE, 0)
    log_col = jnp.log(lax.dynamic_slice_in_dim(col_marg, start, SLICE, 0).astype(jnp.float32))
    log_row = lax.dynamic_update_slice(jnp.zeros((DIM,), jnp.float32), log_col, (xlo * SLICE,))
    pack = jnp.concatenate(
        [embeds, jnp.broadcast_to(log_row[None, :], (PACK - SLICE, DIM))], axis=0
    )
    own = lax.all_to_all(jnp.broadcast_to(pack[None], (8, PACK, DIM)), "z", 0, 0)
    slices = [own] + [fetch(own, move) for move in (x_pair, x_next, x_far)]

    r_own, r_oth, g_own, g_pair, g_next, g_far = cells(where, counts, counts_oth, rb, rb_oth, slices)

    g = g_own + fetch(g_pair, x_pair) + fetch(g_next, x_next) + fetch(g_far, x_far)
    row_grad = (r_own + fetch(r_oth, core_swap)) * (1.0 / 64.0)
    g = lax.all_to_all(g.reshape(64, 8, DIM), ("z", "y"), 0, 0)
    g = jnp.sum(g, axis=0) * (1.0 / math.sqrt(131072.0))
    col_grad = lax.all_to_all(jnp.broadcast_to(g[None], (32, 8, DIM)), ("core", "xlo", "y"), 0, 0)
    return row_grad, col_grad.reshape(256, DIM)


def solution(mesh):
    fine = Mesh(mesh.devices.reshape(SIZES), AXES)
    both = ("xlo", "y", "core", "z", "xhi")
    col = ("z", "xhi")
    return jax.shard_map(
        body,
        mesh=fine,
        in_specs=(P(both, None), P(both), P(col), P(), P(both, None), P(col, None)),
        out_specs=(P(both, None), P(col, None)),
        check_vma=False,
    )
```

```python
import functools
import math

import jax
import jax.numpy as jnp
import numpy as np
from jax import lax
from jax.experimental import pallas as pl
from jax.experimental.pallas import tpu as pltpu
from jax.sharding import Mesh, PartitionSpec as P

AXES = ("xlo", "y", "core", "z", "xhi")
SIZES = (2, 8, 2, 8, 2)
DIM = 256
ROWS = 256
SLICE = 64
PACK = 72
GROUP = 4


def pairs_to(move):
    pairs = []
    for target in range(math.prod(SIZES)):
        at = dict(zip(AXES, (int(i) for i in np.unravel_index(target, SIZES))))
        at.update(move(at))
        pairs.append((int(np.ravel_multi_index([at[a] for a in AXES], SIZES)), target))
    return pairs


def core_swap(at):
    return {"core": 1 - at["core"]}


def x_pair(at):
    return {"xlo": 1 - at["xlo"]}


def x_next(at):
    return {"xlo": 1 - at["xlo"], "xhi": 1 - at["xhi"]}


def side_a(at):
    return x_next(at) if at["core"] else x_pair(at)


def side_b(at):
    return x_pair(at) if at["core"] else x_next(at)


def fetch(value, move):
    return lax.ppermute(value, AXES, pairs_to(move))


def split(value):
    high = value.astype(jnp.bfloat16)
    return high, (value - high.astype(jnp.float32)).astype(jnp.bfloat16)


def dot3(a, b, dims):
    one = functools.partial(
        lax.dot_general, dimension_numbers=(dims, ((), ())), preferred_element_type=jnp.float32
    )
    return one(a[0], b[0]) + (one(a[0], b[1]) + one(a[1], b[0]))


def rows_kernel(rb_own, rb_oth, rh, rl, th, tl):
    for k, ref in enumerate((rb_own, rb_oth)):
        part = slice(k * ROWS, (k + 1) * ROWS)
        value = ref[:, :DIM]
        rh[part, :], rl[part, :] = split(value)
        th[:, part], tl[:, part] = split(value.T)


def prepare_rows(rb_own, rb_oth):
    tall = jax.ShapeDtypeStruct((2 * ROWS, DIM), jnp.bfloat16)
    wide = jax.ShapeDtypeStruct((DIM, 2 * ROWS), jnp.bfloat16)
    return pl.pallas_call(
        rows_kernel,
        out_shape=[tall, tall, wide, wide],
        compiler_params=pltpu.CompilerParams(vmem_limit_bytes=16 * 2**20),
        cost_estimate=pl.CostEstimate(flops=2**22, bytes_accessed=2**21, transcendentals=0),
    )(rb_own, rb_oth)


def cells_kernel(adds_r, adds_g, where, *refs):
    counts = (refs[:GROUP], refs[GROUP : 2 * GROUP])
    rb, (rh, rl, th, tl, pack) = refs[8:10], refs[10:15]
    rest = list(refs[15:])
    r_in = (rest.pop(0), rest.pop(0)) if adds_r else None
    g_in = rest.pop(0) if adds_g else None
    r_out, g_out = rest[:2], rest[2]
    step = pl.program_id(0)

    @pl.when(step == 0)
    def _():
        for k in range(2):
            r_out[k][...] = r_in[k][...] if adds_r else jnp.zeros_like(r_out[k])

    xlo = where[2]
    near, far = xlo * SLICE, (1 - xlo) * SLICE
    e = split(pack[:, :SLICE, :].reshape(GROUP * SLICE, DIM))
    half = lax.broadcasted_iota(jnp.int32, (ROWS, 128), 1) < SLICE
    logs = [pack[i, SLICE : SLICE + 1, :128] for i in range(GROUP)]
    log_col = jnp.concatenate(
        [jnp.where(half[:1], logs[i], logs[i + 1]) for i in (0, 2)], axis=1
    )
    total = None
    for k in range(2):
        part = slice(k * ROWS, (k + 1) * ROWS)
        score = dot3((rh[part, :], rl[part, :]), e, ((1,), (1,)))
        gap = score - rb[k][:, DIM : DIM + 1] + log_col
        cnt = jnp.concatenate(
            [
                jnp.where(
                    half,
                    pltpu.roll(counts[k][i][...], near, 1),
                    pltpu.roll(counts[k][i + 1][...], far, 1),
                )
                for i in (0, 2)
            ],
            axis=1,
        )
        x = cnt.astype(jnp.float32)
        weight = 0.1 + 0.25 * jnp.sqrt(x)
        cell = jnp.where(
            cnt > 0,
            weight * (gap - jnp.log(jnp.maximum(x, 1.0))),
            1.0 / (1.0 + jnp.exp(-gap)),
        )
        cell = split(cell)
        r_out[k][...] += dot3(cell, e, ((1,), (0,)))
        term = dot3((th[:, part], tl[:, part]), cell, ((1,), (0,)))
        total = term if total is None else total + term
    total = total.T.reshape(GROUP, SLICE, DIM)
    g_out[...] = total + g_in[...] if adds_g else total


def cells(where, counts, rows, pack, r_in=None, g_in=None):
    def block(i):
        return pl.BlockSpec((ROWS, 128), lambda j, w: (0, (j * GROUP + i) * 4 + w[1] * 2 + w[0]))

    def whole(shape):
        return pl.BlockSpec(shape, lambda j, w: (0, 0))

    f32 = jnp.float32
    tall, wide = whole((2 * ROWS, DIM)), whole((DIM, 2 * ROWS))
    r_spec = whole((ROWS, DIM))
    g_spec = pl.BlockSpec((GROUP, SLICE, DIM), lambda j, w: (j, 0, 0))
    rb_spec = whole((ROWS, DIM + 128))
    in_specs = [block(i) for i in range(GROUP)] * 2 + [rb_spec] * 2 + [tall, tall, wide, wide]
    in_specs.append(pl.BlockSpec((GROUP, PACK, DIM), lambda j, w: (j, 0, 0)))
    args = [counts[0]] * GROUP + [counts[1]] * GROUP + list(rows) + [pack]
    if r_in is not None:
        in_specs += [r_spec] * 2
        args += list(r_in)
    if g_in is not None:
        in_specs.append(g_spec)
        args.append(g_in)
    r_one, r_two, g = pl.pallas_call(
        functools.partial(cells_kernel, r_in is not None, g_in is not None),
        grid_spec=pltpu.PrefetchScalarGridSpec(
            num_scalar_prefetch=1,
            grid=(8 // GROUP,),
            in_specs=in_specs,
            out_specs=[r_spec] * 2 + [g_spec],
        ),
        out_shape=[jax.ShapeDtypeStruct((ROWS, DIM), f32)] * 2
        + [jax.ShapeDtypeStruct((8, SLICE, DIM), f32)],
        compiler_params=pltpu.CompilerParams(vmem_limit_bytes=50 * 2**20),
        cost_estimate=pl.CostEstimate(
            flops=4 * 10**9, bytes_accessed=4 * 2**20, transcendentals=2**20
        ),
    )(where, *args)
    return (r_one, r_two), g


def body(counts, row_marg, col_marg, log_total, row_embed, col_embed):
    core, xlo, xhi = (lax.axis_index(a) for a in ("core", "xlo", "xhi"))

    def slice_at(hi, lo):
        return jnp.stack([core, hi, lo]).astype(jnp.int32)

    at_own = slice_at(xhi, xlo)
    at_a = slice_at(jnp.where(core == 0, xhi, 1 - xhi), 1 - xlo)
    at_b = slice_at(jnp.where(core == 0, 1 - xhi, xhi), 1 - xlo)
    at_far = slice_at(1 - xhi, xlo)

    start = (core * 2 + xlo) * SLICE
    embeds = lax.dynamic_slice_in_dim(col_embed, start, SLICE, 0)
    log_col = jnp.log(lax.dynamic_slice_in_dim(col_marg, start, SLICE, 0).astype(jnp.float32))
    log_row = jnp.concatenate([log_col] * 4)
    pack = jnp.concatenate(
        [embeds, jnp.broadcast_to(log_row[None, :], (PACK - SLICE, DIM))], axis=0
    )
    s_own = lax.all_to_all(jnp.broadcast_to(pack[None], (8, PACK, DIM)), "z", 0, 0)

    counts = (counts, fetch(counts, core_swap))
    base_row = log_total[0] - jnp.log(row_marg.astype(jnp.float32))
    rb = jnp.concatenate([row_embed, jnp.broadcast_to(base_row[:, None], (ROWS, 128))], axis=1)
    rb_oth = fetch(rb, core_swap)
    rows = (rb, rb_oth, *prepare_rows(rb, rb_oth))
    s_own, rows = lax.optimization_barrier((s_own, rows))

    s_a, s_b = fetch(s_own, side_a), fetch(s_own, side_b)
    r, g_own = cells(at_own, counts, rows, s_own)
    sent = fetch(g_own, side_b)
    s_far = fetch(s_a, side_b)
    r, g_a = cells(at_a, counts, rows, s_a, r)
    from_a = fetch(g_a, side_b)
    r, g_b = cells(at_b, counts, rows, s_b, r, sent)
    from_b = fetch(g_b, side_a)
    r, g = cells(at_far, counts, rows, s_far, r)
    g = g + from_a + from_b

    g = lax.all_to_all(g.reshape(64, 8, DIM), ("z", "y"), 0, 0)
    row_grad = (r[0] + fetch(r[1], core_swap)) * (1.0 / 64.0)
    g = jnp.sum(g, axis=0) * (1.0 / math.sqrt(131072.0))
    g = fetch(g, x_next)
    g = lax.all_to_all(jnp.broadcast_to(g[None], (32, 8, DIM)), ("core", "xlo", "y"), 0, 0)
    g = g.reshape(2, 2, SLICE, DIM)
    col_grad = jnp.stack([g[:, 1], g[:, 0]], axis=1)
    return row_grad, col_grad.reshape(256, DIM)


def solution(mesh):
    fine = Mesh(mesh.devices.reshape(SIZES), AXES)
    both = ("xlo", "y", "core", "z", "xhi")
    col = ("z", "xhi")
    return jax.shard_map(
        body,
        mesh=fine,
        in_specs=(P(both, None), P(both), P(col), P(), P(both, None), P(col, None)),
        out_specs=(P(both, None), P(col, None)),
        check_vma=False,
    )
```

```python
import functools
import math

import jax
import jax.numpy as jnp
import numpy as np
from jax import lax
from jax.experimental import pallas as pl
from jax.experimental.pallas import tpu as pltpu
from jax.sharding import Mesh, PartitionSpec as P

AXES = ("xlo", "y", "core", "z", "xhi")
SIZES = (2, 8, 2, 8, 2)
DIM = 256
ROWS = 256
SLICE = 64
PACK = 72
STRIP = 64
GROUP = 4


def pairs_to(move):
    pairs = []
    for target in range(math.prod(SIZES)):
        at = dict(zip(AXES, (int(i) for i in np.unravel_index(target, SIZES))))
        at.update(move(at))
        pairs.append((int(np.ravel_multi_index([at[a] for a in AXES], SIZES)), target))
    return pairs


def x_far(at):
    return {"xhi": 1 - at["xhi"]}


def core_swap(at):
    return {"core": 1 - at["core"]}


def x_pair(at):
    return {"xlo": 1 - at["xlo"]}


def x_next(at):
    return {"xlo": 1 - at["xlo"], "xhi": 1 - at["xhi"]}


def side_a(at):
    return x_next(at) if at["core"] else x_pair(at)


def side_b(at):
    return x_pair(at) if at["core"] else x_next(at)


def fetch(value, move):
    return lax.ppermute(value, AXES, pairs_to(move))


def split(value):
    high = value.astype(jnp.bfloat16)
    return high, (value - high.astype(jnp.float32)).astype(jnp.bfloat16)


def dot(a, b, dims):
    return lax.dot_general(
        a, b, dimension_numbers=(dims, ((), ())), preferred_element_type=jnp.float32
    )


def left(pair, axis):
    return jnp.concatenate([pair[0], pair[0], pair[1]], axis=axis)


def right(pair, axis):
    return jnp.concatenate([pair[0], pair[1], pair[0]], axis=axis)


def pack_kernel(embed, marg, out):
    start = (2 * lax.axis_index("core") + lax.axis_index("xlo")) * SLICE
    out[:, :SLICE, :] = jnp.broadcast_to(
        embed[pl.ds(pl.multiple_of(start, SLICE), SLICE), :][None], (8, SLICE, DIM)
    )
    logs = jnp.log(marg[...].astype(jnp.float32))
    out[:, SLICE:, :] = jnp.broadcast_to(logs[None], (8, PACK - SLICE, DIM))


def pack_slice(col_embed, col_marg):
    return pl.pallas_call(
        pack_kernel,
        out_shape=jax.ShapeDtypeStruct((8, PACK, DIM), jnp.float32),
        compiler_params=pltpu.CompilerParams(vmem_limit_bytes=60 * 2**20),
    )(col_embed, col_marg.reshape(1, DIM))


def prepare_kernel(table, c_own, c_oth, rb_own, rb_oth, *outs):
    weight_out, shift_out, tall_out, wide_out = outs[:4], outs[4:8], outs[8], outs[9]
    step = pl.program_id(0)
    steps = pl.num_programs(0)

    @pl.when(step == 0)
    def _():
        for k, rb in enumerate((rb_own, rb_oth)):
            part = slice(k * ROWS, (k + 1) * ROWS)
            value = rb[:, :DIM]
            tall_out[part, :] = left(split(value), 1)
            wide = split(value.T)
            for n, source in enumerate((wide[0], wide[0], wide[1])):
                start = n * 2 * ROWS + k * ROWS
                wide_out[:, start : start + ROWS] = source

    def work(counts, rb, block):
        half = lax.broadcasted_iota(jnp.int32, (STRIP, 128), 1) < SLICE
        base = rb[pl.ds(pl.multiple_of(block * STRIP, STRIP), STRIP), DIM:]
        for which in range(4):
            core, xhi, xlo = (table[which * 3 + i] for i in range(3))
            near, far = xlo * SLICE, (1 - xlo) * SLICE
            for n in range(4):
                tiles = [
                    counts[:, pl.ds(pl.multiple_of((z * 4 + xhi * 2 + core) * 128, 128), 128)]
                    for z in (2 * n, 2 * n + 1)
                ]
                cnt = jnp.where(half, pltpu.roll(tiles[0], near, 1), pltpu.roll(tiles[1], far, 1))
                x = jnp.maximum(cnt, 1).astype(jnp.float32)
                weight = jnp.where(cnt > 0, 0.1 + 0.25 * (x * lax.rsqrt(x)), 0.0)
                weight_out[which][:, n * 128 : (n + 1) * 128] = weight
                shift_out[which][:, n * 128 : (n + 1) * 128] = jnp.log(x) + base

    @pl.when(step < steps // 2)
    def _():
        work(c_own, rb_own, step)

    @pl.when(step >= steps // 2)
    def _():
        work(c_oth, rb_oth, step - steps // 2)


def prepare(table, counts, rb):
    half = ROWS // STRIP

    def whole(shape):
        return pl.BlockSpec(shape, lambda i, w: (0, 0))

    columns = counts[0].shape[1]
    cell_spec = pl.BlockSpec((STRIP, 2 * DIM), lambda i, w: (i, 0))
    cell_shape = jax.ShapeDtypeStruct((2 * ROWS, 2 * DIM), jnp.float32)
    *cell, tall, wide = pl.pallas_call(
        prepare_kernel,
        grid_spec=pltpu.PrefetchScalarGridSpec(
            num_scalar_prefetch=1,
            grid=(2 * half,),
            in_specs=[
                pl.BlockSpec((STRIP, columns), lambda i, w: (jnp.minimum(i, half - 1), 0)),
                pl.BlockSpec((STRIP, columns), lambda i, w: (jnp.maximum(i - half, 0), 0)),
            ]
            + [whole((ROWS, DIM + 128))] * 2,
            out_specs=[cell_spec] * 8 + [whole((2 * ROWS, 3 * DIM)), whole((DIM, 6 * ROWS))],
        ),
        out_shape=[cell_shape] * 8
        + [
            jax.ShapeDtypeStruct((2 * ROWS, 3 * DIM), jnp.bfloat16),
            jax.ShapeDtypeStruct((DIM, 6 * ROWS), jnp.bfloat16),
        ],
        compiler_params=pltpu.CompilerParams(vmem_limit_bytes=48 * 2**20),
        cost_estimate=pl.CostEstimate(flops=4 * 10**9, bytes_accessed=2**23, transcendentals=2**20),
    )(table, *counts, *rb)
    return cell[:4], cell[4:], tall, wide


def cells_kernel(which, adds_r, adds_g, table, weight, shift, tall, wide, pack, *rest):
    rest = list(rest)
    r_in = rest.pop(0) if adds_r else None
    g_in = rest.pop(0) if adds_g else None
    r_out, g_out = rest
    offset = (2 * table[3 * which] + table[3 * which + 2]) * SLICE
    near, far = lax.rem(DIM - offset, DIM), lax.rem(DIM + SLICE - offset, DIM)
    half = lax.broadcasted_iota(jnp.int32, (1, 128), 1) < SLICE
    r_sum = None
    for j in range(8 // GROUP):
        part = slice(j * DIM, (j + 1) * DIM)
        here = pack[j * GROUP : (j + 1) * GROUP]
        e = split(here[:, :SLICE, :].reshape(DIM, DIM))
        logs = [here[i, SLICE : SLICE + 8, :] for i in range(GROUP)]
        log_col = jnp.concatenate(
            [
                jnp.where(
                    half,
                    pltpu.roll(logs[i], near, 1)[:1, :128],
                    pltpu.roll(logs[i + 1], far, 1)[:1, :128],
                )
                for i in (0, 2)
            ],
            axis=1,
        )
        gap = dot(tall[...], right(e, 1), ((1,), (1,))) + log_col - shift[:, part]
        w = weight[:, part]
        cell = split(jnp.where(w > 0.0, w * gap, 0.5 + 0.5 * jnp.tanh(0.5 * gap)))
        r_term = dot(left(cell, 1), right(e, 0), ((1,), (0,)))
        r_sum = r_term if r_sum is None else r_sum + r_term
        total = dot(wide[...], right(cell, 0), ((1,), (0,))).T.reshape(GROUP, SLICE, DIM)
        if adds_g:
            total += g_in[j * GROUP : (j + 1) * GROUP]
        g_out[j * GROUP : (j + 1) * GROUP] = total
    r_out[...] = r_sum + r_in[...] if adds_r else r_sum


def cells(which, table, prepared, pack, r_in=None, g_in=None):
    vmem = pl.BlockSpec(memory_space=pltpu.VMEM)
    weights, shifts, tall, wide = prepared
    args = [weights[which], shifts[which], tall, wide, pack] + [a for a in (r_in, g_in) if a is not None]
    return pl.pallas_call(
        functools.partial(cells_kernel, which, r_in is not None, g_in is not None),
        in_specs=[pl.BlockSpec(memory_space=pltpu.SMEM)] + [vmem] * len(args),
        out_specs=[vmem] * 2,
        out_shape=[
            jax.ShapeDtypeStruct((2 * ROWS, DIM), jnp.float32),
            jax.ShapeDtypeStruct((8, SLICE, DIM), jnp.float32),
        ],
        compiler_params=pltpu.CompilerParams(vmem_limit_bytes=32 * 2**20),
        cost_estimate=pl.CostEstimate(
            flops=3 * 10**9, bytes_accessed=2**22, transcendentals=2**18
        ),
    )(table, *args)


def body(counts, row_marg, col_marg, log_total, row_embed, col_embed):
    core, xlo, xhi = (lax.axis_index(a) for a in ("core", "xlo", "xhi"))
    table = jnp.stack(
        [core, xhi, xlo]
        + [core, jnp.where(core == 0, xhi, 1 - xhi), 1 - xlo]
        + [core, jnp.where(core == 0, 1 - xhi, xhi), 1 - xlo]
        + [core, 1 - xhi, xlo]
    ).astype(jnp.int32)

    pack, row_marg = lax.optimization_barrier((pack_slice(col_embed, col_marg), row_marg))
    s_own = lax.all_to_all(pack, "z", 0, 0)

    base_row = log_total[0] - jnp.log(row_marg.astype(jnp.float32))
    rb = jnp.concatenate([row_embed, jnp.broadcast_to(base_row[:, None], (ROWS, 128))], axis=1)
    rb, counts = lax.optimization_barrier((rb, counts))
    prepared = prepare(table, (counts, fetch(counts, core_swap)), (rb, fetch(rb, core_swap)))
    weights, shifts, tall, wide = prepared
    s_own, tall = lax.optimization_barrier((s_own, tall))
    prepared = (weights, shifts, tall, wide)

    s_a, s_b = fetch(s_own, side_a), fetch(s_own, side_b)
    r, g_own = cells(0, table, prepared, s_own)
    sent = fetch(g_own, side_b)
    s_far = fetch(s_a, side_b)
    r, g_a = cells(1, table, prepared, s_a, r)
    from_a = fetch(g_a, side_b)
    r, g_b = cells(2, table, prepared, s_b, r, sent)
    from_b = fetch(g_b, side_a)
    r, g = cells(3, table, prepared, s_far, r)
    g = g + from_a + from_b

    g = lax.all_to_all(g.reshape(64, 8, DIM), ("z", "y"), 0, 0)
    row_grad = (r[:ROWS] + fetch(r[ROWS:], core_swap)) * (1.0 / 64.0)
    g = jnp.sum(g, axis=0) * (1.0 / math.sqrt(131072.0))
    g = fetch(g, x_far)
    g = lax.all_to_all(jnp.broadcast_to(g[None], (32, 8, DIM)), ("core", "xlo", "y"), 0, 0)
    return row_grad, g.reshape(256, DIM)


def solution(mesh):
    fine = Mesh(mesh.devices.reshape(SIZES), AXES)
    both = ("xlo", "y", "core", "z", "xhi")
    col = ("z", "xhi")
    return jax.shard_map(
        body,
        mesh=fine,
        in_specs=(P(both, None), P(both), P(col), P(), P(both, None), P(col, None)),
        out_specs=(P(both, None), P(col, None)),
        check_vma=False,
    )
```

```python
import functools
import math

import jax
import jax.numpy as jnp
import numpy as np
from jax import lax
from jax.experimental import pallas as pl
from jax.experimental.pallas import tpu as pltpu
from jax.sharding import Mesh, PartitionSpec as P

AXES = ("xlo", "y", "core", "z", "xhi")
SIZES = (2, 8, 2, 8, 2)
DIM = 256
ROWS = 256
SLICE = 64
PACK = 72
STRIP = 64
GROUP = 4


def pairs_to(move):
    pairs = []
    for target in range(math.prod(SIZES)):
        at = dict(zip(AXES, (int(i) for i in np.unravel_index(target, SIZES))))
        at.update(move(at))
        pairs.append((int(np.ravel_multi_index([at[a] for a in AXES], SIZES)), target))
    return pairs


def x_far(at):
    return {"xhi": 1 - at["xhi"]}


def core_swap(at):
    return {"core": 1 - at["core"]}


def x_pair(at):
    return {"xlo": 1 - at["xlo"]}


def x_next(at):
    return {"xlo": 1 - at["xlo"], "xhi": 1 - at["xhi"]}


def side_a(at):
    return x_next(at) if at["core"] else x_pair(at)


def side_b(at):
    return x_pair(at) if at["core"] else x_next(at)


def fetch(value, move):
    return lax.ppermute(value, AXES, pairs_to(move))


def split(value):
    high = value.astype(jnp.bfloat16)
    return high, (value - high.astype(jnp.float32)).astype(jnp.bfloat16)


def dot(a, b, dims):
    return lax.dot_general(
        a, b, dimension_numbers=(dims, ((), ())), preferred_element_type=jnp.float32
    )


def left(pair, axis):
    return jnp.concatenate([pair[0], pair[0], pair[1]], axis=axis)


def right(pair, axis):
    return jnp.concatenate([pair[0], pair[1], pair[0]], axis=axis)


def pack_kernel(embed, marg, out):
    start = (2 * lax.axis_index("core") + lax.axis_index("xlo")) * SLICE
    out[:, :SLICE, :] = jnp.broadcast_to(
        embed[pl.ds(pl.multiple_of(start, SLICE), SLICE), :][None], (8, SLICE, DIM)
    )
    logs = jnp.log(marg[...].astype(jnp.float32))
    out[:, SLICE:, :] = jnp.broadcast_to(logs[None], (8, PACK - SLICE, DIM))


def pack_slice(col_embed, col_marg):
    return pl.pallas_call(
        pack_kernel,
        out_shape=jax.ShapeDtypeStruct((8, PACK, DIM), jnp.float32),
        compiler_params=pltpu.CompilerParams(vmem_limit_bytes=60 * 2**20),
    )(col_embed, col_marg.reshape(1, DIM))


def prepare_kernel(table, c_own, c_oth, rb_own, rb_oth, *outs):
    count_out, (rh, rl, th, tl, base) = outs[:4], outs[4:]
    step = pl.program_id(0)
    steps = pl.num_programs(0)

    @pl.when(step == 0)
    def _():
        for k, rb in enumerate((rb_own, rb_oth)):
            part = slice(k * ROWS, (k + 1) * ROWS)
            value = rb[:, :DIM]
            rh[part, :], rl[part, :] = split(value)
            th[:, part], tl[:, part] = split(value.T)
            base[part, :] = rb[:, DIM:]

    def work(counts):
        half = lax.broadcasted_iota(jnp.int32, (STRIP, 128), 1) < SLICE
        for which in range(4):
            core, xhi, xlo = (table[which * 3 + i] for i in range(3))
            near, far = xlo * SLICE, (1 - xlo) * SLICE
            for n in range(4):
                tiles = [
                    counts[:, pl.ds(pl.multiple_of((z * 4 + xhi * 2 + core) * 128, 128), 128)]
                    for z in (2 * n, 2 * n + 1)
                ]
                cnt = jnp.where(half, pltpu.roll(tiles[0], near, 1), pltpu.roll(tiles[1], far, 1))
                count_out[which][:, n * 128 : (n + 1) * 128] = cnt.astype(jnp.float32)

    @pl.when(step < steps // 2)
    def _():
        work(c_own)

    @pl.when(step >= steps // 2)
    def _():
        work(c_oth)


def prepare(table, counts, rb):
    half = ROWS // STRIP

    def whole(shape):
        return pl.BlockSpec(shape, lambda i, w: (0, 0))

    columns = counts[0].shape[1]
    tall, wide, base = (2 * ROWS, DIM), (DIM, 2 * ROWS), (2 * ROWS, 128)
    bf16 = jnp.bfloat16
    outs = pl.pallas_call(
        prepare_kernel,
        grid_spec=pltpu.PrefetchScalarGridSpec(
            num_scalar_prefetch=1,
            grid=(2 * half,),
            in_specs=[
                pl.BlockSpec((STRIP, columns), lambda i, w: (jnp.minimum(i, half - 1), 0)),
                pl.BlockSpec((STRIP, columns), lambda i, w: (jnp.maximum(i - half, 0), 0)),
            ]
            + [whole((ROWS, DIM + 128))] * 2,
            out_specs=[pl.BlockSpec((STRIP, 2 * DIM), lambda i, w: (i, 0))] * 4
            + [whole(tall)] * 2
            + [whole(wide)] * 2
            + [whole(base)],
        ),
        out_shape=[jax.ShapeDtypeStruct((2 * ROWS, 2 * DIM), jnp.float32)] * 4
        + [jax.ShapeDtypeStruct(tall, bf16)] * 2
        + [jax.ShapeDtypeStruct(wide, bf16)] * 2
        + [jax.ShapeDtypeStruct(base, jnp.float32)],
        compiler_params=pltpu.CompilerParams(vmem_limit_bytes=48 * 2**20),
        cost_estimate=pl.CostEstimate(flops=2**22, bytes_accessed=2**21, transcendentals=0),
    )(table, *counts, *rb)
    return outs[:4], outs[4:]


def cells_kernel(which, adds_r, adds_g, table, count, rh, rl, th, tl, base, pack, *rest):
    rest = list(rest)
    r_in = rest.pop(0) if adds_r else None
    g_in = rest.pop(0) if adds_g else None
    r_out, g_out = rest
    offset = (2 * table[3 * which] + table[3 * which + 2]) * SLICE
    near, far = lax.rem(DIM - offset, DIM), lax.rem(DIM + SLICE - offset, DIM)
    half = lax.broadcasted_iota(jnp.int32, (1, 128), 1) < SLICE
    tall, wide = left((rh[...], rl[...]), 1), left((th[...], tl[...]), 1)
    r_sum = None
    for j in range(8 // GROUP):
        part = slice(j * DIM, (j + 1) * DIM)
        here = pack[j * GROUP : (j + 1) * GROUP]
        e = split(here[:, :SLICE, :].reshape(DIM, DIM))
        logs = [here[i, SLICE : SLICE + 8, :] for i in range(GROUP)]
        log_col = jnp.concatenate(
            [
                jnp.where(
                    half,
                    pltpu.roll(logs[i], near, 1)[:1, :128],
                    pltpu.roll(logs[i + 1], far, 1)[:1, :128],
                )
                for i in (0, 2)
            ],
            axis=1,
        )
        gap = dot(tall, right(e, 1), ((1,), (1,))) + log_col - base[:, :1]
        cnt = count[:, part]
        x = jnp.maximum(cnt, 1.0)
        cell = jnp.where(
            cnt > 0.0,
            (0.1 + 0.25 * (x * lax.rsqrt(x))) * (gap - jnp.log(x)),
            0.5 + 0.5 * jnp.tanh(0.5 * gap),
        )
        cell = split(cell)
        r_term = dot(left(cell, 1), right(e, 0), ((1,), (0,)))
        r_sum = r_term if r_sum is None else r_sum + r_term
        total = dot(wide, right(cell, 0), ((1,), (0,))).T.reshape(GROUP, SLICE, DIM)
        if adds_g:
            total += g_in[j * GROUP : (j + 1) * GROUP]
        g_out[j * GROUP : (j + 1) * GROUP] = total
    r_out[...] = r_sum + r_in[...] if adds_r else r_sum


def cells(which, table, prepared, pack, r_in=None, g_in=None):
    vmem = pl.BlockSpec(memory_space=pltpu.VMEM)
    counts, rows = prepared
    args = [counts[which], *rows, pack] + [a for a in (r_in, g_in) if a is not None]
    return pl.pallas_call(
        functools.partial(cells_kernel, which, r_in is not None, g_in is not None),
        in_specs=[pl.BlockSpec(memory_space=pltpu.SMEM)] + [vmem] * len(args),
        out_specs=[vmem] * 2,
        out_shape=[
            jax.ShapeDtypeStruct((2 * ROWS, DIM), jnp.float32),
            jax.ShapeDtypeStruct((8, SLICE, DIM), jnp.float32),
        ],
        compiler_params=pltpu.CompilerParams(vmem_limit_bytes=32 * 2**20),
        cost_estimate=pl.CostEstimate(
            flops=4 * 10**9, bytes_accessed=4 * 2**20, transcendentals=2**20
        ),
    )(table, *args)


def body(counts, row_marg, col_marg, log_total, row_embed, col_embed):
    core, xlo, xhi = (lax.axis_index(a) for a in ("core", "xlo", "xhi"))
    table = jnp.stack(
        [core, xhi, xlo]
        + [core, jnp.where(core == 0, xhi, 1 - xhi), 1 - xlo]
        + [core, jnp.where(core == 0, 1 - xhi, xhi), 1 - xlo]
        + [core, 1 - xhi, xlo]
    ).astype(jnp.int32)

    s_own = lax.all_to_all(pack_slice(col_embed, col_marg), "z", 0, 0)
    base_row = log_total[0] - jnp.log(row_marg.astype(jnp.float32))
    rb = jnp.concatenate([row_embed, jnp.broadcast_to(base_row[:, None], (ROWS, 128))], axis=1)
    s_own, rb, rb_oth, counts_oth = lax.optimization_barrier(
        (s_own, rb, fetch(rb, core_swap), fetch(counts, core_swap))
    )
    prepared = prepare(table, (counts, counts_oth), (rb, rb_oth))

    s_a, s_b = fetch(s_own, side_a), fetch(s_own, side_b)
    r, g_own = cells(0, table, prepared, s_own)
    sent = fetch(g_own, side_b)
    s_far = fetch(s_a, side_b)
    r, g_a = cells(1, table, prepared, s_a, r)
    from_a = fetch(g_a, side_b)
    r, g_b = cells(2, table, prepared, s_b, r, sent)
    from_b = fetch(g_b, side_a)
    r, g = cells(3, table, prepared, s_far, r)
    g = g + from_a + from_b

    g = lax.all_to_all(g.reshape(64, 8, DIM), ("z", "y"), 0, 0)
    row_grad = (r[:ROWS] + fetch(r[ROWS:], core_swap)) * (1.0 / 64.0)
    g = jnp.sum(g, axis=0) * (1.0 / math.sqrt(131072.0))
    g = fetch(g, x_far)
    g = lax.all_to_all(jnp.broadcast_to(g[None], (32, 8, DIM)), ("core", "xlo", "y"), 0, 0)
    return row_grad, g.reshape(256, DIM)


def solution(mesh):
    fine = Mesh(mesh.devices.reshape(SIZES), AXES)
    both = ("xlo", "y", "core", "z", "xhi")
    col = ("z", "xhi")
    return jax.shard_map(
        body,
        mesh=fine,
        in_specs=(P(both, None), P(both), P(col), P(), P(both, None), P(col, None)),
        out_specs=(P(both, None), P(col, None)),
        check_vma=False,
    )
```

```python
import functools
import math

import jax
import jax.numpy as jnp
import numpy as np
from jax import lax
from jax.experimental import pallas as pl
from jax.experimental.pallas import tpu as pltpu
from jax.sharding import Mesh, PartitionSpec as P

AXES = ("xlo", "y", "core", "z", "xhi")
SIZES = (2, 8, 2, 8, 2)
DIM = 256
ROWS = 256
SLICE = 64
PACK = 72
STRIP = 64
GROUP = 4


def pairs_to(move):
    pairs = []
    for target in range(math.prod(SIZES)):
        at = dict(zip(AXES, (int(i) for i in np.unravel_index(target, SIZES))))
        at.update(move(at))
        pairs.append((int(np.ravel_multi_index([at[a] for a in AXES], SIZES)), target))
    return pairs


def x_far(at):
    return {"xhi": 1 - at["xhi"]}


def core_swap(at):
    return {"core": 1 - at["core"]}


def x_pair(at):
    return {"xlo": 1 - at["xlo"]}


def x_next(at):
    return {"xlo": 1 - at["xlo"], "xhi": 1 - at["xhi"]}


def side_a(at):
    return x_next(at) if at["core"] else x_pair(at)


def side_b(at):
    return x_pair(at) if at["core"] else x_next(at)


def fetch(value, move):
    return lax.ppermute(value, AXES, pairs_to(move))


def split(value):
    high = value.astype(jnp.bfloat16)
    return high, (value - high.astype(jnp.float32)).astype(jnp.bfloat16)


def dot(a, b, dims):
    return lax.dot_general(
        a, b, dimension_numbers=(dims, ((), ())), preferred_element_type=jnp.float32
    )


def left(pair, axis):
    return jnp.concatenate([pair[0], pair[0], pair[1]], axis=axis)


def right(pair, axis):
    return jnp.concatenate([pair[0], pair[1], pair[0]], axis=axis)


def pack_kernel(embed, marg, out):
    start = (2 * lax.axis_index("core") + lax.axis_index("xlo")) * SLICE
    out[:, :SLICE, :] = jnp.broadcast_to(
        embed[pl.ds(pl.multiple_of(start, SLICE), SLICE), :][None], (8, SLICE, DIM)
    )
    logs = jnp.log(marg[...].astype(jnp.float32))
    out[:, SLICE:, :] = jnp.broadcast_to(logs[None], (8, PACK - SLICE, DIM))


def pack_slice(col_embed, col_marg):
    return pl.pallas_call(
        pack_kernel,
        out_shape=jax.ShapeDtypeStruct((8, PACK, DIM), jnp.float32),
        compiler_params=pltpu.CompilerParams(vmem_limit_bytes=60 * 2**20),
    )(col_embed, col_marg.reshape(1, DIM))


def rows_kernel(rb_own, rb_oth, rh, rl, th, tl, base):
    for k, rb in enumerate((rb_own, rb_oth)):
        part = slice(k * ROWS, (k + 1) * ROWS)
        value = rb[:, :DIM]
        rh[part, :], rl[part, :] = split(value)
        th[:, part], tl[:, part] = split(value.T)
        base[part, :] = rb[:, DIM:]


def prepare_rows(rb_own, rb_oth):
    tall = jax.ShapeDtypeStruct((2 * ROWS, DIM), jnp.bfloat16)
    wide = jax.ShapeDtypeStruct((DIM, 2 * ROWS), jnp.bfloat16)
    base = jax.ShapeDtypeStruct((2 * ROWS, 128), jnp.float32)
    vmem = pl.BlockSpec(memory_space=pltpu.VMEM)
    return pl.pallas_call(
        rows_kernel,
        in_specs=[vmem] * 2,
        out_specs=[vmem] * 5,
        out_shape=[tall, tall, wide, wide, base],
        compiler_params=pltpu.CompilerParams(vmem_limit_bytes=16 * 2**20),
        cost_estimate=pl.CostEstimate(flops=2**22, bytes_accessed=2**21, transcendentals=0),
    )(rb_own, rb_oth)


def counts_kernel(table, c_own, c_oth, *count_out):
    step = pl.program_id(0)
    steps = pl.num_programs(0)

    def work(counts):
        half = lax.broadcasted_iota(jnp.int32, (STRIP, 128), 1) < SLICE
        for which in range(4):
            core, xhi, xlo = (table[which * 3 + i] for i in range(3))
            near, far = xlo * SLICE, (1 - xlo) * SLICE
            for n in range(4):
                tiles = [
                    counts[:, pl.ds(pl.multiple_of((z * 4 + xhi * 2 + core) * 128, 128), 128)]
                    for z in (2 * n, 2 * n + 1)
                ]
                cnt = jnp.where(half, pltpu.roll(tiles[0], near, 1), pltpu.roll(tiles[1], far, 1))
                count_out[which][:, n * 128 : (n + 1) * 128] = cnt.astype(jnp.float32)

    @pl.when(step < steps // 2)
    def _():
        work(c_own)

    @pl.when(step >= steps // 2)
    def _():
        work(c_oth)


def prepare_counts(table, counts):
    half = ROWS // STRIP
    columns = counts[0].shape[1]
    return pl.pallas_call(
        counts_kernel,
        grid_spec=pltpu.PrefetchScalarGridSpec(
            num_scalar_prefetch=1,
            grid=(2 * half,),
            in_specs=[
                pl.BlockSpec((STRIP, columns), lambda i, w: (jnp.minimum(i, half - 1), 0)),
                pl.BlockSpec((STRIP, columns), lambda i, w: (jnp.maximum(i - half, 0), 0)),
            ],
            out_specs=[pl.BlockSpec((STRIP, 2 * DIM), lambda i, w: (i, 0))] * 4,
        ),
        out_shape=[jax.ShapeDtypeStruct((2 * ROWS, 2 * DIM), jnp.float32)] * 4,
        compiler_params=pltpu.CompilerParams(vmem_limit_bytes=54 * 2**20),
        cost_estimate=pl.CostEstimate(flops=2**22, bytes_accessed=2**21, transcendentals=0),
    )(table, *counts)


def cells_kernel(which, adds_r, adds_g, table, count, rh, rl, th, tl, base, pack, *rest):
    rest = list(rest)
    r_in = rest.pop(0) if adds_r else None
    g_in = rest.pop(0) if adds_g else None
    r_out, g_out = rest
    offset = (2 * table[3 * which] + table[3 * which + 2]) * SLICE
    near, far = lax.rem(DIM - offset, DIM), lax.rem(DIM + SLICE - offset, DIM)
    half = lax.broadcasted_iota(jnp.int32, (1, 128), 1) < SLICE
    tall, wide = left((rh[...], rl[...]), 1), left((th[...], tl[...]), 1)
    r_sum = None
    for j in range(8 // GROUP):
        part = slice(j * DIM, (j + 1) * DIM)
        here = pack[j * GROUP : (j + 1) * GROUP]
        e = split(here[:, :SLICE, :].reshape(DIM, DIM))
        logs = [here[i, SLICE : SLICE + 8, :] for i in range(GROUP)]
        log_col = jnp.concatenate(
            [
                jnp.where(
                    half,
                    pltpu.roll(logs[i], near, 1)[:1, :128],
                    pltpu.roll(logs[i + 1], far, 1)[:1, :128],
                )
                for i in (0, 2)
            ],
            axis=1,
        )
        gap = dot(tall, right(e, 1), ((1,), (1,))) + log_col - base[:, :1]
        cnt = count[:, part]
        x = jnp.maximum(cnt, 1.0)
        cell = jnp.where(
            cnt > 0.0,
            (0.1 + 0.25 * (x * lax.rsqrt(x))) * (gap - jnp.log(x)),
            0.5 + 0.5 * jnp.tanh(0.5 * gap),
        )
        cell = split(cell)
        r_term = dot(left(cell, 1), right(e, 0), ((1,), (0,)))
        r_sum = r_term if r_sum is None else r_sum + r_term
        total = dot(wide, right(cell, 0), ((1,), (0,))).T.reshape(GROUP, SLICE, DIM)
        if adds_g:
            total += g_in[j * GROUP : (j + 1) * GROUP]
        g_out[j * GROUP : (j + 1) * GROUP] = total
    r_out[...] = r_sum + r_in[...] if adds_r else r_sum


def cells(which, table, prepared, pack, r_in=None, g_in=None):
    vmem = pl.BlockSpec(memory_space=pltpu.VMEM)
    counts, rows = prepared
    args = [counts[which], *rows, pack] + [a for a in (r_in, g_in) if a is not None]
    return pl.pallas_call(
        functools.partial(cells_kernel, which, r_in is not None, g_in is not None),
        in_specs=[pl.BlockSpec(memory_space=pltpu.SMEM)] + [vmem] * len(args),
        out_specs=[vmem] * 2,
        out_shape=[
            jax.ShapeDtypeStruct((2 * ROWS, DIM), jnp.float32),
            jax.ShapeDtypeStruct((8, SLICE, DIM), jnp.float32),
        ],
        compiler_params=pltpu.CompilerParams(vmem_limit_bytes=32 * 2**20),
        cost_estimate=pl.CostEstimate(
            flops=4 * 10**9, bytes_accessed=4 * 2**20, transcendentals=2**20
        ),
    )(table, *args)


def body(counts, row_marg, col_marg, log_total, row_embed, col_embed):
    core, xlo, xhi = (lax.axis_index(a) for a in ("core", "xlo", "xhi"))
    table = jnp.stack(
        [core, xhi, xlo]
        + [core, jnp.where(core == 0, xhi, 1 - xhi), 1 - xlo]
        + [core, jnp.where(core == 0, 1 - xhi, xhi), 1 - xlo]
        + [core, 1 - xhi, xlo]
    ).astype(jnp.int32)

    s_own = lax.all_to_all(pack_slice(col_embed, col_marg), "z", 0, 0)
    base_row = log_total[0] - jnp.log(row_marg.astype(jnp.float32))
    rb = jnp.concatenate([row_embed, jnp.broadcast_to(base_row[:, None], (ROWS, 128))], axis=1)
    by_slice = prepare_counts(table, (counts, fetch(counts, core_swap)))
    s_own, rb, rb_oth, by_slice = lax.optimization_barrier(
        (s_own, rb, fetch(rb, core_swap), by_slice)
    )
    prepared = (by_slice, prepare_rows(rb, rb_oth))

    s_a, s_b = fetch(s_own, side_a), fetch(s_own, side_b)
    r, g_own = cells(0, table, prepared, s_own)
    sent = fetch(g_own, side_b)
    s_far = fetch(s_a, side_b)
    r, g_a = cells(1, table, prepared, s_a, r)
    from_a = fetch(g_a, side_b)
    r, g_b = cells(2, table, prepared, s_b, r, sent)
    from_b = fetch(g_b, side_a)
    r, g = cells(3, table, prepared, s_far, r, from_a)
    g = g + from_b

    g = lax.all_to_all(g.reshape(64, 8, DIM), ("z", "y"), 0, 0)
    row_grad = (r[:ROWS] + fetch(r[ROWS:], core_swap)) * (1.0 / 64.0)
    g = jnp.sum(g, axis=0) * (1.0 / math.sqrt(131072.0))
    g = fetch(g, x_far)
    g = lax.all_to_all(jnp.broadcast_to(g[None], (32, 8, DIM)), ("core", "xlo", "y"), 0, 0)
    return row_grad, g.reshape(256, DIM)


def solution(mesh):
    fine = Mesh(mesh.devices.reshape(SIZES), AXES)
    both = ("xlo", "y", "core", "z", "xhi")
    col = ("z", "xhi")
    return jax.shard_map(
        body,
        mesh=fine,
        in_specs=(P(both, None), P(both), P(col), P(), P(both, None), P(col, None)),
        out_specs=(P(both, None), P(col, None)),
        check_vma=False,
    )
```

```python
import functools
import math

import jax
import jax.numpy as jnp
import numpy as np
from jax import lax
from jax.experimental import pallas as pl
from jax.experimental.pallas import tpu as pltpu
from jax.sharding import Mesh, PartitionSpec as P

AXES = ("xlo", "y", "core", "z", "xhi")
SIZES = (2, 8, 2, 8, 2)
DIM = 256
ROWS = 256
SLICE = 64
PACK = 72
STRIP = 64
GROUP = 4


def pairs_to(move):
    pairs = []
    for target in range(math.prod(SIZES)):
        at = dict(zip(AXES, (int(i) for i in np.unravel_index(target, SIZES))))
        at.update(move(at))
        pairs.append((int(np.ravel_multi_index([at[a] for a in AXES], SIZES)), target))
    return pairs


def core_swap(at):
    return {"core": 1 - at["core"]}


def x_pair(at):
    return {"xlo": 1 - at["xlo"]}


def x_next(at):
    return {"xlo": 1 - at["xlo"], "xhi": 1 - at["xhi"]}


def x_next_core(at):
    return {**x_next(at), **core_swap(at)}


def side_a(at):
    return x_next(at) if at["core"] else x_pair(at)


def side_b(at):
    return x_pair(at) if at["core"] else x_next(at)


def fetch(value, move):
    return lax.ppermute(value, AXES, pairs_to(move))


def split(value):
    high = value.astype(jnp.bfloat16)
    return high, (value - high.astype(jnp.float32)).astype(jnp.bfloat16)


def dot(a, b, dims):
    return lax.dot_general(
        a, b, dimension_numbers=(dims, ((), ())), preferred_element_type=jnp.float32
    )


def left(pair, axis):
    return jnp.concatenate([pair[0], pair[0], pair[1]], axis=axis)


def right(pair, axis):
    return jnp.concatenate([pair[0], pair[1], pair[0]], axis=axis)


def pack_kernel(embed, marg, out):
    start = (2 * lax.axis_index("core") + lax.axis_index("xlo")) * SLICE
    out[:, :SLICE, :] = jnp.broadcast_to(
        embed[pl.ds(pl.multiple_of(start, SLICE), SLICE), :][None], (8, SLICE, DIM)
    )
    logs = jnp.log(marg[...].astype(jnp.float32))
    out[:, SLICE:, :] = jnp.broadcast_to(logs[None], (8, PACK - SLICE, DIM))


def pack_slice(col_embed, col_marg):
    return pl.pallas_call(
        pack_kernel,
        out_shape=jax.ShapeDtypeStruct((8, PACK, DIM), jnp.float32),
        compiler_params=pltpu.CompilerParams(vmem_limit_bytes=60 * 2**20),
    )(col_embed, col_marg.reshape(1, DIM))


def rows_kernel(rb_own, rb_oth, rh, rl, th, tl, base):
    for k, rb in enumerate((rb_own, rb_oth)):
        part = slice(k * ROWS, (k + 1) * ROWS)
        value = rb[:, :DIM]
        rh[part, :], rl[part, :] = split(value)
        th[:, part], tl[:, part] = split(value.T)
        base[part, :] = rb[:, DIM:]


def prepare_rows(rb_own, rb_oth):
    tall = jax.ShapeDtypeStruct((2 * ROWS, DIM), jnp.bfloat16)
    wide = jax.ShapeDtypeStruct((DIM, 2 * ROWS), jnp.bfloat16)
    base = jax.ShapeDtypeStruct((2 * ROWS, 128), jnp.float32)
    vmem = pl.BlockSpec(memory_space=pltpu.VMEM)
    return pl.pallas_call(
        rows_kernel,
        in_specs=[vmem] * 2,
        out_specs=[vmem] * 5,
        out_shape=[tall, tall, wide, wide, base],
        compiler_params=pltpu.CompilerParams(vmem_limit_bytes=16 * 2**20),
        cost_estimate=pl.CostEstimate(flops=2**22, bytes_accessed=2**21, transcendentals=0),
    )(rb_own, rb_oth)


def counts_kernel(table, c_own, c_oth, *count_out):
    step = pl.program_id(0)
    steps = pl.num_programs(0)

    def work(counts):
        half = lax.broadcasted_iota(jnp.int32, (STRIP, 128), 1) < SLICE
        for which in range(4):
            core, xhi, xlo = (table[which * 3 + i] for i in range(3))
            near, far = xlo * SLICE, (1 - xlo) * SLICE
            for n in range(4):
                tiles = [
                    counts[:, pl.ds(pl.multiple_of((z * 4 + xhi * 2 + core) * 128, 128), 128)]
                    for z in (2 * n, 2 * n + 1)
                ]
                cnt = jnp.where(half, pltpu.roll(tiles[0], near, 1), pltpu.roll(tiles[1], far, 1))
                count_out[which][:, n * 128 : (n + 1) * 128] = cnt.astype(jnp.float32)

    @pl.when(step < steps // 2)
    def _():
        work(c_own)

    @pl.when(step >= steps // 2)
    def _():
        work(c_oth)


def prepare_counts(table, counts):
    half = ROWS // STRIP
    columns = counts[0].shape[1]
    return pl.pallas_call(
        counts_kernel,
        grid_spec=pltpu.PrefetchScalarGridSpec(
            num_scalar_prefetch=1,
            grid=(2 * half,),
            in_specs=[
                pl.BlockSpec((STRIP, columns), lambda i, w: (jnp.minimum(i, half - 1), 0)),
                pl.BlockSpec((STRIP, columns), lambda i, w: (jnp.maximum(i - half, 0), 0)),
            ],
            out_specs=[pl.BlockSpec((STRIP, 2 * DIM), lambda i, w: (i, 0))] * 4,
        ),
        out_shape=[jax.ShapeDtypeStruct((2 * ROWS, 2 * DIM), jnp.float32)] * 4,
        compiler_params=pltpu.CompilerParams(vmem_limit_bytes=54 * 2**20),
        cost_estimate=pl.CostEstimate(flops=2**22, bytes_accessed=2**21, transcendentals=0),
    )(table, *counts)


def cells_kernel(which, adds_r, adds_g, table, count, rh, rl, th, tl, base, pack, *rest):
    rest = list(rest)
    r_in = rest.pop(0) if adds_r else None
    g_in = rest.pop(0) if adds_g else None
    r_out, g_out = rest
    offset = (2 * table[3 * which] + table[3 * which + 2]) * SLICE
    near, far = lax.rem(DIM - offset, DIM), lax.rem(DIM + SLICE - offset, DIM)
    half = lax.broadcasted_iota(jnp.int32, (1, 128), 1) < SLICE
    tall, wide = left((rh[...], rl[...]), 1), left((th[...], tl[...]), 1)
    r_sum = None
    for j in range(8 // GROUP):
        part = slice(j * DIM, (j + 1) * DIM)
        here = pack[j * GROUP : (j + 1) * GROUP]
        e = split(here[:, :SLICE, :].reshape(DIM, DIM))
        logs = [here[i, SLICE : SLICE + 8, :] for i in range(GROUP)]
        log_col = jnp.concatenate(
            [
                jnp.where(
                    half,
                    pltpu.roll(logs[i], near, 1)[:1, :128],
                    pltpu.roll(logs[i + 1], far, 1)[:1, :128],
                )
                for i in (0, 2)
            ],
            axis=1,
        )
        gap = dot(tall, right(e, 1), ((1,), (1,))) + log_col - base[:, :1]
        cnt = count[:, part]
        x = jnp.maximum(cnt, 1.0)
        cell = jnp.where(
            cnt > 0.0,
            (0.1 + 0.25 * (x * lax.rsqrt(x))) * (gap - jnp.log(x)),
            0.5 + 0.5 * jnp.tanh(0.5 * gap),
        )
        cell = split(cell)
        r_term = dot(left(cell, 1), right(e, 0), ((1,), (0,)))
        r_sum = r_term if r_sum is None else r_sum + r_term
        total = dot(wide, right(cell, 0), ((1,), (0,))).T.reshape(GROUP, SLICE, DIM)
        if adds_g:
            total += g_in[j * GROUP : (j + 1) * GROUP]
        g_out[j * GROUP : (j + 1) * GROUP] = total
    r_out[...] = r_sum + r_in[...] if adds_r else r_sum


def cells(which, table, prepared, pack, r_in=None, g_in=None):
    vmem = pl.BlockSpec(memory_space=pltpu.VMEM)
    counts, rows = prepared
    args = [counts[which], *rows, pack] + [a for a in (r_in, g_in) if a is not None]
    return pl.pallas_call(
        functools.partial(cells_kernel, which, r_in is not None, g_in is not None),
        in_specs=[pl.BlockSpec(memory_space=pltpu.SMEM)] + [vmem] * len(args),
        out_specs=[vmem] * 2,
        out_shape=[
            jax.ShapeDtypeStruct((2 * ROWS, DIM), jnp.float32),
            jax.ShapeDtypeStruct((8, SLICE, DIM), jnp.float32),
        ],
        compiler_params=pltpu.CompilerParams(vmem_limit_bytes=32 * 2**20),
        cost_estimate=pl.CostEstimate(
            flops=4 * 10**9, bytes_accessed=4 * 2**20, transcendentals=2**20
        ),
    )(table, *args)


def body(counts, row_marg, col_marg, log_total, row_embed, col_embed):
    core, xlo, xhi = (lax.axis_index(a) for a in ("core", "xlo", "xhi"))
    table = jnp.stack(
        [core, xhi, xlo]
        + [core, jnp.where(core == 0, xhi, 1 - xhi), 1 - xlo]
        + [core, jnp.where(core == 0, 1 - xhi, xhi), 1 - xlo]
        + [core, 1 - xhi, xlo]
    ).astype(jnp.int32)

    s_own = lax.all_to_all(pack_slice(col_embed, col_marg), "z", 0, 0)
    base_row = log_total[0] - jnp.log(row_marg.astype(jnp.float32))
    rb = jnp.concatenate([row_embed, jnp.broadcast_to(base_row[:, None], (ROWS, 128))], axis=1)
    by_slice = prepare_counts(table, (counts, fetch(counts, core_swap)))
    s_own, rb, rb_oth, by_slice = lax.optimization_barrier(
        (s_own, rb, fetch(rb, core_swap), by_slice)
    )
    prepared = (by_slice, prepare_rows(rb, rb_oth))

    s_a, s_b = fetch(s_own, side_a), fetch(s_own, side_b)
    r, g_own = cells(0, table, prepared, s_own)
    sent = fetch(g_own, side_b)
    s_far = fetch(s_a, side_b)
    r, g_a = cells(1, table, prepared, s_a, r)
    from_a = fetch(g_a, side_b)
    r, g_b = cells(2, table, prepared, s_b, r, sent)
    from_b = fetch(g_b, side_a)
    r, g = cells(3, table, prepared, s_far, r)
    g = lax.optimization_barrier(g + from_a) + from_b

    g = lax.all_to_all(g.reshape(64, 8, DIM), ("z", "y"), 0, 0)
    row_grad = (r[:ROWS] + fetch(r[ROWS:], core_swap)) * (1.0 / 64.0)
    g = jnp.sum(g, axis=0) * (1.0 / math.sqrt(131072.0))
    g = lax.all_to_all(jnp.broadcast_to(g[None], (16, 8, DIM)), ("xlo", "y"), 0, 0)
    g = g.reshape(2 * SLICE, DIM)
    same, other = fetch(g, x_next), fetch(g, x_next_core)
    col_grad = jnp.where(
        core == 0, jnp.concatenate([same, other]), jnp.concatenate([other, same])
    )
    return row_grad, col_grad


def solution(mesh):
    fine = Mesh(mesh.devices.reshape(SIZES), AXES)
    both = ("xlo", "y", "core", "z", "xhi")
    col = ("z", "xhi")
    return jax.shard_map(
        body,
        mesh=fine,
        in_specs=(P(both, None), P(both), P(col), P(), P(both, None), P(col, None)),
        out_specs=(P(both, None), P(col, None)),
        check_vma=False,
    )
```

```python
import functools
import math

import jax
import jax.numpy as jnp
import numpy as np
from jax import lax
from jax.experimental import pallas as pl
from jax.experimental.pallas import tpu as pltpu
from jax.sharding import Mesh, PartitionSpec as P

AXES = ("xlo", "y", "core", "z", "xhi")
SIZES = (2, 8, 2, 8, 2)
DIM = 256
ROWS = 256
SLICE = 64
PACK = 72
STRIP = 64
GROUP = 4


def pairs_to(move):
    pairs = []
    for target in range(math.prod(SIZES)):
        at = dict(zip(AXES, (int(i) for i in np.unravel_index(target, SIZES))))
        at.update(move(at))
        pairs.append((int(np.ravel_multi_index([at[a] for a in AXES], SIZES)), target))
    return pairs


def x_far(at):
    return {"xhi": 1 - at["xhi"]}


def core_swap(at):
    return {"core": 1 - at["core"]}


def x_pair(at):
    return {"xlo": 1 - at["xlo"]}


def x_next(at):
    return {"xlo": 1 - at["xlo"], "xhi": 1 - at["xhi"]}


def side_a(at):
    return x_next(at) if at["core"] else x_pair(at)


def side_b(at):
    return x_pair(at) if at["core"] else x_next(at)


def fetch(value, move):
    return lax.ppermute(value, AXES, pairs_to(move))


def split(value):
    high = value.astype(jnp.bfloat16)
    return high, (value - high.astype(jnp.float32)).astype(jnp.bfloat16)


def dot(a, b, dims):
    return lax.dot_general(
        a, b, dimension_numbers=(dims, ((), ())), preferred_element_type=jnp.float32
    )


def left(pair, axis):
    return jnp.concatenate([pair[0], pair[0], pair[1]], axis=axis)


def right(pair, axis):
    return jnp.concatenate([pair[0], pair[1], pair[0]], axis=axis)


def pack_kernel(embed, marg, out):
    start = (2 * lax.axis_index("core") + lax.axis_index("xlo")) * SLICE
    out[:, :SLICE, :] = jnp.broadcast_to(
        embed[pl.ds(pl.multiple_of(start, SLICE), SLICE), :][None], (8, SLICE, DIM)
    )
    logs = jnp.log(marg[...].astype(jnp.float32))
    out[:, SLICE:, :] = jnp.broadcast_to(logs[None], (8, PACK - SLICE, DIM))


def pack_slice(col_embed, col_marg):
    return pl.pallas_call(
        pack_kernel,
        out_shape=jax.ShapeDtypeStruct((8, PACK, DIM), jnp.float32),
        compiler_params=pltpu.CompilerParams(vmem_limit_bytes=60 * 2**20),
    )(col_embed, col_marg.reshape(1, DIM))


def rows_kernel(rb_own, rb_oth, rh, rl, th, tl, base):
    for k, rb in enumerate((rb_own, rb_oth)):
        part = slice(k * ROWS, (k + 1) * ROWS)
        value = rb[:, :DIM]
        rh[part, :], rl[part, :] = split(value)
        th[:, part], tl[:, part] = split(value.T)
        base[part, :] = rb[:, DIM:]


def prepare_rows(rb_own, rb_oth):
    tall = jax.ShapeDtypeStruct((2 * ROWS, DIM), jnp.bfloat16)
    wide = jax.ShapeDtypeStruct((DIM, 2 * ROWS), jnp.bfloat16)
    base = jax.ShapeDtypeStruct((2 * ROWS, 128), jnp.float32)
    vmem = pl.BlockSpec(memory_space=pltpu.VMEM)
    return pl.pallas_call(
        rows_kernel,
        in_specs=[vmem] * 2,
        out_specs=[vmem] * 5,
        out_shape=[tall, tall, wide, wide, base],
        compiler_params=pltpu.CompilerParams(vmem_limit_bytes=16 * 2**20),
        cost_estimate=pl.CostEstimate(flops=2**22, bytes_accessed=2**21, transcendentals=0),
    )(rb_own, rb_oth)


def counts_kernel(table, c_own, c_oth, *count_out):
    step = pl.program_id(0)
    steps = pl.num_programs(0)

    def work(counts):
        half = lax.broadcasted_iota(jnp.int32, (STRIP, 128), 1) < SLICE
        for which in range(4):
            core, xhi, xlo = (table[which * 3 + i] for i in range(3))
            near, far = xlo * SLICE, (1 - xlo) * SLICE
            for n in range(4):
                tiles = [
                    counts[:, pl.ds(pl.multiple_of((z * 4 + xhi * 2 + core) * 128, 128), 128)]
                    for z in (2 * n, 2 * n + 1)
                ]
                cnt = jnp.where(half, pltpu.roll(tiles[0], near, 1), pltpu.roll(tiles[1], far, 1))
                count_out[which][:, n * 128 : (n + 1) * 128] = cnt.astype(jnp.float32)

    @pl.when(step < steps // 2)
    def _():
        work(c_own)

    @pl.when(step >= steps // 2)
    def _():
        work(c_oth)


def prepare_counts(table, counts):
    half = ROWS // STRIP
    columns = counts[0].shape[1]
    return pl.pallas_call(
        counts_kernel,
        grid_spec=pltpu.PrefetchScalarGridSpec(
            num_scalar_prefetch=1,
            grid=(2 * half,),
            in_specs=[
                pl.BlockSpec((STRIP, columns), lambda i, w: (jnp.minimum(i, half - 1), 0)),
                pl.BlockSpec((STRIP, columns), lambda i, w: (jnp.maximum(i - half, 0), 0)),
            ],
            out_specs=[pl.BlockSpec((STRIP, 2 * DIM), lambda i, w: (i, 0))] * 4,
        ),
        out_shape=[jax.ShapeDtypeStruct((2 * ROWS, 2 * DIM), jnp.float32)] * 4,
        compiler_params=pltpu.CompilerParams(vmem_limit_bytes=54 * 2**20),
        cost_estimate=pl.CostEstimate(flops=2**22, bytes_accessed=2**21, transcendentals=0),
    )(table, *counts)


def cells_kernel(which, adds_r, adds_g, table, count, rh, rl, th, tl, base, pack, *rest):
    rest = list(rest)
    r_in = rest.pop(0) if adds_r else None
    g_in = rest.pop(0) if adds_g else None
    r_out, g_out = rest
    offset = (2 * table[3 * which] + table[3 * which + 2]) * SLICE
    near, far = lax.rem(DIM - offset, DIM), lax.rem(DIM + SLICE - offset, DIM)
    half = lax.broadcasted_iota(jnp.int32, (1, 128), 1) < SLICE
    tall, wide = left((rh[...], rl[...]), 1), left((th[...], tl[...]), 1)
    r_sum = None
    for j in range(8 // GROUP):
        part = slice(j * DIM, (j + 1) * DIM)
        here = pack[j * GROUP : (j + 1) * GROUP]
        e = split(here[:, :SLICE, :].reshape(DIM, DIM))
        logs = [here[i, SLICE : SLICE + 8, :] for i in range(GROUP)]
        log_col = jnp.concatenate(
            [
                jnp.where(
                    half,
                    pltpu.roll(logs[i], near, 1)[:1, :128],
                    pltpu.roll(logs[i + 1], far, 1)[:1, :128],
                )
                for i in (0, 2)
            ],
            axis=1,
        )
        gap = dot(tall, right(e, 1), ((1,), (1,))) + log_col - base[:, :1]
        cnt = count[:, part]
        x = jnp.maximum(cnt, 1.0)
        cell = jnp.where(
            cnt > 0.0,
            (0.1 + 0.25 * (x * lax.rsqrt(x))) * (gap - jnp.log(x)),
            0.5 + 0.5 * jnp.tanh(0.5 * gap),
        )
        cell = split(cell)
        r_term = dot(left(cell, 1), right(e, 0), ((1,), (0,)))
        r_sum = r_term if r_sum is None else r_sum + r_term
        total = dot(wide, right(cell, 0), ((1,), (0,))).T.reshape(GROUP, SLICE, DIM)
        if adds_g:
            total += g_in[j * GROUP : (j + 1) * GROUP]
        g_out[j * GROUP : (j + 1) * GROUP] = total
    r_out[...] = r_sum + r_in[...] if adds_r else r_sum


def cells(which, table, prepared, pack, r_in=None, g_in=None):
    vmem = pl.BlockSpec(memory_space=pltpu.VMEM)
    counts, rows = prepared
    args = [counts[which], *rows, pack] + [a for a in (r_in, g_in) if a is not None]
    return pl.pallas_call(
        functools.partial(cells_kernel, which, r_in is not None, g_in is not None),
        in_specs=[pl.BlockSpec(memory_space=pltpu.SMEM)] + [vmem] * len(args),
        out_specs=[vmem] * 2,
        out_shape=[
            jax.ShapeDtypeStruct((2 * ROWS, DIM), jnp.float32),
            jax.ShapeDtypeStruct((8, SLICE, DIM), jnp.float32),
        ],
        compiler_params=pltpu.CompilerParams(vmem_limit_bytes=32 * 2**20),
        cost_estimate=pl.CostEstimate(
            flops=4 * 10**9, bytes_accessed=4 * 2**20, transcendentals=2**20
        ),
    )(table, *args)


def body(counts, row_marg, col_marg, log_total, row_embed, col_embed):
    core, xlo, xhi = (lax.axis_index(a) for a in ("core", "xlo", "xhi"))
    table = jnp.stack(
        [core, xhi, xlo]
        + [core, jnp.where(core == 0, xhi, 1 - xhi), 1 - xlo]
        + [core, jnp.where(core == 0, 1 - xhi, xhi), 1 - xlo]
        + [core, 1 - xhi, xlo]
    ).astype(jnp.int32)

    s_own = lax.all_to_all(pack_slice(col_embed, col_marg), "z", 0, 0)
    base_row = log_total[0] - jnp.log(row_marg.astype(jnp.float32))
    rb = jnp.concatenate([row_embed, jnp.broadcast_to(base_row[:, None], (ROWS, 128))], axis=1)
    by_slice = prepare_counts(table, (counts, fetch(counts, core_swap)))
    s_own, rb, rb_oth, by_slice = lax.optimization_barrier(
        (s_own, rb, fetch(rb, core_swap), by_slice)
    )
    prepared = (by_slice, prepare_rows(rb, rb_oth))

    s_a = fetch(s_own, side_a)
    r, g_own = cells(0, table, prepared, s_own)
    s_own, g_own = lax.optimization_barrier((s_own, g_own))
    s_b = fetch(s_own, side_b)
    sent = fetch(g_own, side_b)
    s_far = fetch(s_a, side_b)
    r, g_a = cells(1, table, prepared, s_a, r)
    from_a = fetch(g_a, side_b)
    r, g_b = cells(2, table, prepared, s_b, r, sent)
    from_b = fetch(g_b, side_a)
    r, g = cells(3, table, prepared, s_far, r)
    g = lax.optimization_barrier(g + from_a) + from_b

    g = lax.all_to_all(g.reshape(64, 8, DIM), ("z", "y"), 0, 0)
    row_grad = (r[:ROWS] + fetch(r[ROWS:], core_swap)) * (1.0 / 64.0)
    g = jnp.sum(g, axis=0) * (1.0 / math.sqrt(131072.0))
    g = fetch(g, x_far)
    g = lax.all_to_all(jnp.broadcast_to(g[None], (32, 8, DIM)), ("core", "xlo", "y"), 0, 0)
    return row_grad, g.reshape(256, DIM)


def solution(mesh):
    fine = Mesh(mesh.devices.reshape(SIZES), AXES)
    both = ("xlo", "y", "core", "z", "xhi")
    col = ("z", "xhi")
    return jax.shard_map(
        body,
        mesh=fine,
        in_specs=(P(both, None), P(both), P(col), P(), P(both, None), P(col, None)),
        out_specs=(P(both, None), P(col, None)),
        check_vma=False,
    )
```

```python
import functools
import math

import jax
import jax.numpy as jnp
import numpy as np
from jax import lax
from jax.experimental import pallas as pl
from jax.experimental.pallas import tpu as pltpu
from jax.sharding import Mesh, PartitionSpec as P

AXES = ("xlo", "y", "core", "z", "xhi")
SIZES = (2, 8, 2, 8, 2)
DIM = 256
ROWS = 256
SLICE = 64
PACK = 72
STRIP = 64
PARITY = 12
GROUP = 4


def pairs_to(move):
    pairs = []
    for target in range(math.prod(SIZES)):
        at = dict(zip(AXES, (int(i) for i in np.unravel_index(target, SIZES))))
        at.update(move(at))
        pairs.append((int(np.ravel_multi_index([at[a] for a in AXES], SIZES)), target))
    return pairs


def x_far(at):
    return {"xhi": 1 - at["xhi"]}


def core_swap(at):
    return {"core": 1 - at["core"]}


def x_pair(at):
    return {"xlo": 1 - at["xlo"]}


def x_next(at):
    return {"xlo": 1 - at["xlo"], "xhi": 1 - at["xhi"]}


def side_a(at):
    return x_next(at) if at["core"] else x_pair(at)


def side_b(at):
    return x_pair(at) if at["core"] else x_next(at)


def y_pair(at):
    return {"y": at["y"] ^ 1}


def fetch(value, move):
    return lax.ppermute(value, AXES, pairs_to(move))


def split(value):
    high = value.astype(jnp.bfloat16)
    return high, (value - high.astype(jnp.float32)).astype(jnp.bfloat16)


def dot(a, b, dims):
    return lax.dot_general(
        a, b, dimension_numbers=(dims, ((), ())), preferred_element_type=jnp.float32
    )


def left(pair, axis):
    return jnp.concatenate([pair[0], pair[0], pair[1]], axis=axis)


def right(pair, axis):
    return jnp.concatenate([pair[0], pair[1], pair[0]], axis=axis)


def pack_kernel(embed, marg, out):
    start = (2 * lax.axis_index("core") + lax.axis_index("xlo")) * SLICE
    out[:, :SLICE, :] = jnp.broadcast_to(
        embed[pl.ds(pl.multiple_of(start, SLICE), SLICE), :][None], (8, SLICE, DIM)
    )
    logs = jnp.log(marg[...].astype(jnp.float32))
    out[:, SLICE:, :] = jnp.broadcast_to(logs[None], (8, PACK - SLICE, DIM))


def pack_slice(col_embed, col_marg):
    return pl.pallas_call(
        pack_kernel,
        out_shape=jax.ShapeDtypeStruct((8, PACK, DIM), jnp.float32),
        compiler_params=pltpu.CompilerParams(vmem_limit_bytes=60 * 2**20),
    )(col_embed, col_marg.reshape(1, DIM))


def rows_kernel(rb_own, rb_oth, rh, rl, th, tl, base):
    for k, rb in enumerate((rb_own, rb_oth)):
        part = slice(k * ROWS, (k + 1) * ROWS)
        value = rb[:, :DIM]
        rh[part, :], rl[part, :] = split(value)
        th[:, part], tl[:, part] = split(value.T)
        base[part, :] = rb[:, DIM:]


def prepare_rows(rb_own, rb_oth):
    tall = jax.ShapeDtypeStruct((2 * ROWS, DIM), jnp.bfloat16)
    wide = jax.ShapeDtypeStruct((DIM, 2 * ROWS), jnp.bfloat16)
    base = jax.ShapeDtypeStruct((2 * ROWS, 128), jnp.float32)
    vmem = pl.BlockSpec(memory_space=pltpu.VMEM)
    return pl.pallas_call(
        rows_kernel,
        in_specs=[vmem] * 2,
        out_specs=[vmem] * 5,
        out_shape=[tall, tall, wide, wide, base],
        compiler_params=pltpu.CompilerParams(vmem_limit_bytes=16 * 2**20),
        cost_estimate=pl.CostEstimate(flops=2**22, bytes_accessed=2**21, transcendentals=0),
    )(rb_own, rb_oth)


def counts_kernel(table, c_own, c_oth, *count_out):
    step = pl.program_id(0)
    steps = pl.num_programs(0)

    def work(counts):
        half = lax.broadcasted_iota(jnp.int32, (STRIP, 128), 1) < SLICE
        for which in range(4):
            core, xhi, xlo = (table[which * 3 + i] for i in range(3))
            near, far = xlo * SLICE, (1 - xlo) * SLICE
            for n in range(4):
                tiles = [
                    counts[:, pl.ds(pl.multiple_of((z * 4 + xhi * 2 + core) * 128, 128), 128)]
                    for z in (2 * n, 2 * n + 1)
                ]
                cnt = jnp.where(half, pltpu.roll(tiles[0], near, 1), pltpu.roll(tiles[1], far, 1))
                count_out[which][:, n * 128 : (n + 1) * 128] = cnt.astype(jnp.float32)

    @pl.when(step < steps // 2)
    def _():
        work(c_own)

    @pl.when(step >= steps // 2)
    def _():
        work(c_oth)


def prepare_counts(table, counts):
    half = ROWS // STRIP
    columns = counts[0].shape[1]
    return pl.pallas_call(
        counts_kernel,
        grid_spec=pltpu.PrefetchScalarGridSpec(
            num_scalar_prefetch=1,
            grid=(2 * half,),
            in_specs=[
                pl.BlockSpec((STRIP, columns), lambda i, w: (jnp.minimum(i, half - 1), 0)),
                pl.BlockSpec((STRIP, columns), lambda i, w: (jnp.maximum(i - half, 0), 0)),
            ],
            out_specs=[pl.BlockSpec((STRIP, 2 * DIM), lambda i, w: (i, 0))] * 4,
        ),
        out_shape=[jax.ShapeDtypeStruct((2 * ROWS, 2 * DIM), jnp.float32)] * 4,
        compiler_params=pltpu.CompilerParams(vmem_limit_bytes=54 * 2**20),
        cost_estimate=pl.CostEstimate(flops=2**22, bytes_accessed=2**21, transcendentals=0),
    )(table, *counts)


def half_kernel(table, pack, out):
    out[...] = jnp.where(table[PARITY] == 0, pack[:GROUP], pack[GROUP:])


def half_of(table, pack):
    vmem = pl.BlockSpec(memory_space=pltpu.VMEM)
    return pl.pallas_call(
        half_kernel,
        in_specs=[pl.BlockSpec(memory_space=pltpu.SMEM), vmem],
        out_specs=vmem,
        out_shape=jax.ShapeDtypeStruct((GROUP, PACK, DIM), jnp.float32),
        compiler_params=pltpu.CompilerParams(vmem_limit_bytes=8 * 2**20),
    )(table, pack)


def cells_kernel(which, halves, adds_r, adds_g, table, count, rh, rl, th, tl, base, *rest):
    rest = list(rest)
    pack = rest.pop(0)
    pack_more = rest.pop(0) if halves else None
    r_in = rest.pop(0) if adds_r else None
    g_in = rest.pop(0) if adds_g else None
    r_out, g_out = rest
    offset = (2 * table[3 * which] + table[3 * which + 2]) * SLICE
    near, far = lax.rem(DIM - offset, DIM), lax.rem(DIM + SLICE - offset, DIM)
    half = lax.broadcasted_iota(jnp.int32, (1, 128), 1) < SLICE
    tall, wide = left((rh[...], rl[...]), 1), left((th[...], tl[...]), 1)
    r_sum = None
    for j in range(8 // GROUP):
        part = slice(j * DIM, (j + 1) * DIM)
        if halves:
            here = jnp.where(table[PARITY] == j, pack[...], pack_more[...])
        else:
            here = pack[j * GROUP : (j + 1) * GROUP]
        e = split(here[:, :SLICE, :].reshape(DIM, DIM))
        logs = [here[i, SLICE : SLICE + 8, :] for i in range(GROUP)]
        log_col = jnp.concatenate(
            [
                jnp.where(
                    half,
                    pltpu.roll(logs[i], near, 1)[:1, :128],
                    pltpu.roll(logs[i + 1], far, 1)[:1, :128],
                )
                for i in (0, 2)
            ],
            axis=1,
        )
        gap = dot(tall, right(e, 1), ((1,), (1,))) + log_col - base[:, :1]
        cnt = count[:, part]
        x = jnp.maximum(cnt, 1.0)
        cell = jnp.where(
            cnt > 0.0,
            (0.1 + 0.25 * (x * lax.rsqrt(x))) * (gap - jnp.log(x)),
            0.5 + 0.5 * jnp.tanh(0.5 * gap),
        )
        cell = split(cell)
        r_term = dot(left(cell, 1), right(e, 0), ((1,), (0,)))
        r_sum = r_term if r_sum is None else r_sum + r_term
        total = dot(wide, right(cell, 0), ((1,), (0,))).T.reshape(GROUP, SLICE, DIM)
        if adds_g:
            total += g_in[j * GROUP : (j + 1) * GROUP]
        g_out[j * GROUP : (j + 1) * GROUP] = total
    r_out[...] = r_sum + r_in[...] if adds_r else r_sum


def cells(which, table, prepared, pack, r_in=None, g_in=None):
    vmem = pl.BlockSpec(memory_space=pltpu.VMEM)
    counts, rows = prepared
    args = [counts[which], *rows, *pack] + [a for a in (r_in, g_in) if a is not None]
    return pl.pallas_call(
        functools.partial(cells_kernel, which, len(pack) == 2, r_in is not None, g_in is not None),
        in_specs=[pl.BlockSpec(memory_space=pltpu.SMEM)] + [vmem] * len(args),
        out_specs=[vmem] * 2,
        out_shape=[
            jax.ShapeDtypeStruct((2 * ROWS, DIM), jnp.float32),
            jax.ShapeDtypeStruct((8, SLICE, DIM), jnp.float32),
        ],
        compiler_params=pltpu.CompilerParams(vmem_limit_bytes=32 * 2**20),
        cost_estimate=pl.CostEstimate(
            flops=4 * 10**9, bytes_accessed=4 * 2**20, transcendentals=2**20
        ),
    )(table, *args)


def body(counts, row_marg, col_marg, log_total, row_embed, col_embed):
    core, xlo, xhi = (lax.axis_index(a) for a in ("core", "xlo", "xhi"))
    parity = lax.axis_index("y") % 2
    table = jnp.stack(
        [core, xhi, xlo]
        + [core, jnp.where(core == 0, xhi, 1 - xhi), 1 - xlo]
        + [core, jnp.where(core == 0, 1 - xhi, xhi), 1 - xlo]
        + [core, 1 - xhi, xlo, parity]
    ).astype(jnp.int32)

    s_own = lax.all_to_all(pack_slice(col_embed, col_marg), "z", 0, 0)
    base_row = log_total[0] - jnp.log(row_marg.astype(jnp.float32))
    rb = jnp.concatenate([row_embed, jnp.broadcast_to(base_row[:, None], (ROWS, 128))], axis=1)
    by_slice = prepare_counts(table, (counts, fetch(counts, core_swap)))
    s_own, rb, rb_oth, by_slice = lax.optimization_barrier(
        (s_own, rb, fetch(rb, core_swap), by_slice)
    )
    prepared = (by_slice, prepare_rows(rb, rb_oth))

    s_a, s_b = fetch(s_own, side_a), fetch(s_own, side_b)
    r, g_own = cells(0, table, prepared, [s_own])
    sent = fetch(g_own, side_b)
    s_far = fetch(half_of(table, s_a), side_b)
    s_more = fetch(s_far, y_pair)
    r, g_a = cells(1, table, prepared, [s_a], r)
    from_a = fetch(g_a, side_b)
    r, g_b = cells(2, table, prepared, [s_b], r, sent)
    from_b = fetch(g_b, side_a)
    r, g = cells(3, table, prepared, [s_far, s_more], r, from_a)
    g = g + from_b

    g = lax.all_to_all(g.reshape(64, 8, DIM), ("z", "y"), 0, 0)
    row_grad = (r[:ROWS] + fetch(r[ROWS:], core_swap)) * (1.0 / 64.0)
    g = jnp.sum(g, axis=0) * (1.0 / math.sqrt(131072.0))
    g = fetch(g, x_far)
    g = lax.all_to_all(jnp.broadcast_to(g[None], (32, 8, DIM)), ("core", "xlo", "y"), 0, 0)
    return row_grad, g.reshape(256, DIM)


def solution(mesh):
    fine = Mesh(mesh.devices.reshape(SIZES), AXES)
    both = ("xlo", "y", "core", "z", "xhi")
    col = ("z", "xhi")
    return jax.shard_map(
        body,
        mesh=fine,
        in_specs=(P(both, None), P(both), P(col), P(), P(both, None), P(col, None)),
        out_specs=(P(both, None), P(col, None)),
        check_vma=False,
    )
```

```python
import functools
import math

import jax
import jax.numpy as jnp
import numpy as np
from jax import lax
from jax.experimental import pallas as pl
from jax.experimental.pallas import tpu as pltpu
from jax.sharding import Mesh, PartitionSpec as P

AXES = ("xlo", "y", "core", "z", "xhi")
SIZES = (2, 8, 2, 8, 2)
DIM = 256
ROWS = 256
SLICE = 64
PACK = 72
STRIP = 64
GROUP = 4


def pairs_to(move):
    pairs = []
    for target in range(math.prod(SIZES)):
        at = dict(zip(AXES, (int(i) for i in np.unravel_index(target, SIZES))))
        at.update(move(at))
        pairs.append((int(np.ravel_multi_index([at[a] for a in AXES], SIZES)), target))
    return pairs


def x_far(at):
    return {"xhi": 1 - at["xhi"]}


def core_swap(at):
    return {"core": 1 - at["core"]}


def x_pair(at):
    return {"xlo": 1 - at["xlo"]}


def x_next(at):
    return {"xlo": 1 - at["xlo"], "xhi": 1 - at["xhi"]}


def side_a(at):
    return x_next(at) if at["core"] else x_pair(at)


def side_b(at):
    return x_pair(at) if at["core"] else x_next(at)


def fetch(value, move):
    return lax.ppermute(value, AXES, pairs_to(move))


def split(value):
    high = value.astype(jnp.bfloat16)
    return high, (value - high.astype(jnp.float32)).astype(jnp.bfloat16)


def dot(a, b, dims):
    return lax.dot_general(
        a, b, dimension_numbers=(dims, ((), ())), preferred_element_type=jnp.float32
    )


def left(pair, axis):
    return jnp.concatenate([pair[0], pair[0], pair[1]], axis=axis)


def right(pair, axis):
    return jnp.concatenate([pair[0], pair[1], pair[0]], axis=axis)


def pack_kernel(embed, marg, out):
    start = (2 * lax.axis_index("core") + lax.axis_index("xlo")) * SLICE
    out[:, :SLICE, :] = jnp.broadcast_to(
        embed[pl.ds(pl.multiple_of(start, SLICE), SLICE), :][None], (8, SLICE, DIM)
    )
    logs = jnp.log(marg[...].astype(jnp.float32))
    out[:, SLICE:, :] = jnp.broadcast_to(logs[None], (8, PACK - SLICE, DIM))


def pack_slice(col_embed, col_marg):
    return pl.pallas_call(
        pack_kernel,
        out_shape=jax.ShapeDtypeStruct((8, PACK, DIM), jnp.float32),
        compiler_params=pltpu.CompilerParams(vmem_limit_bytes=60 * 2**20),
    )(col_embed, col_marg.reshape(1, DIM))


def rows_kernel(rb_own, rb_oth, rh, rl, th, tl, base):
    for k, rb in enumerate((rb_own, rb_oth)):
        part = slice(k * ROWS, (k + 1) * ROWS)
        value = rb[:, :DIM]
        rh[part, :], rl[part, :] = split(value)
        th[:, part], tl[:, part] = split(value.T)
        base[part, :] = rb[:, DIM:]


def prepare_rows(rb_own, rb_oth):
    tall = jax.ShapeDtypeStruct((2 * ROWS, DIM), jnp.bfloat16)
    wide = jax.ShapeDtypeStruct((DIM, 2 * ROWS), jnp.bfloat16)
    base = jax.ShapeDtypeStruct((2 * ROWS, 128), jnp.float32)
    vmem = pl.BlockSpec(memory_space=pltpu.VMEM)
    return pl.pallas_call(
        rows_kernel,
        in_specs=[vmem] * 2,
        out_specs=[vmem] * 5,
        out_shape=[tall, tall, wide, wide, base],
        compiler_params=pltpu.CompilerParams(vmem_limit_bytes=16 * 2**20),
        cost_estimate=pl.CostEstimate(flops=2**22, bytes_accessed=2**21, transcendentals=0),
    )(rb_own, rb_oth)


def counts_kernel(table, c_own, c_oth, *count_out):
    step = pl.program_id(0)
    steps = pl.num_programs(0)

    def work(counts):
        half = lax.broadcasted_iota(jnp.int32, (STRIP, 128), 1) < SLICE
        for which in range(4):
            core, xhi, xlo = (table[which * 3 + i] for i in range(3))
            near, far = xlo * SLICE, (1 - xlo) * SLICE
            for n in range(4):
                tiles = [
                    counts[:, pl.ds(pl.multiple_of((z * 4 + xhi * 2 + core) * 128, 128), 128)]
                    for z in (2 * n, 2 * n + 1)
                ]
                cnt = jnp.where(half, pltpu.roll(tiles[0], near, 1), pltpu.roll(tiles[1], far, 1))
                count_out[which][:, n * 128 : (n + 1) * 128] = cnt.astype(jnp.float32)

    @pl.when(step < steps // 2)
    def _():
        work(c_own)

    @pl.when(step >= steps // 2)
    def _():
        work(c_oth)


def prepare_counts(table, counts):
    half = ROWS // STRIP
    columns = counts[0].shape[1]
    return pl.pallas_call(
        counts_kernel,
        grid_spec=pltpu.PrefetchScalarGridSpec(
            num_scalar_prefetch=1,
            grid=(2 * half,),
            in_specs=[
                pl.BlockSpec((STRIP, columns), lambda i, w: (jnp.minimum(i, half - 1), 0)),
                pl.BlockSpec((STRIP, columns), lambda i, w: (jnp.maximum(i - half, 0), 0)),
            ],
            out_specs=[pl.BlockSpec((STRIP, 2 * DIM), lambda i, w: (i, 0))] * 4,
        ),
        out_shape=[jax.ShapeDtypeStruct((2 * ROWS, 2 * DIM), jnp.float32)] * 4,
        compiler_params=pltpu.CompilerParams(vmem_limit_bytes=54 * 2**20),
        cost_estimate=pl.CostEstimate(flops=2**22, bytes_accessed=2**21, transcendentals=0),
    )(table, *counts)


def cells_kernel(which, adds_r, adds_g, table, count, rh, rl, th, tl, base, pack, *rest):
    rest = list(rest)
    r_in = rest.pop(0) if adds_r else None
    g_in = rest.pop(0) if adds_g else None
    r_out, g_out = rest
    offset = (2 * table[3 * which] + table[3 * which + 2]) * SLICE
    near, far = lax.rem(DIM - offset, DIM), lax.rem(DIM + SLICE - offset, DIM)
    half = lax.broadcasted_iota(jnp.int32, (1, 128), 1) < SLICE
    tall, wide = left((rh[...], rl[...]), 1), left((th[...], tl[...]), 1)
    r_sum = None
    for j in range(8 // GROUP):
        part = slice(j * DIM, (j + 1) * DIM)
        here = pack[j * GROUP : (j + 1) * GROUP]
        e = split(here[:, :SLICE, :].reshape(DIM, DIM))
        logs = [here[i, SLICE : SLICE + 8, :] for i in range(GROUP)]
        log_col = jnp.concatenate(
            [
                jnp.where(
                    half,
                    pltpu.roll(logs[i], near, 1)[:1, :128],
                    pltpu.roll(logs[i + 1], far, 1)[:1, :128],
                )
                for i in (0, 2)
            ],
            axis=1,
        )
        gap = dot(tall, right(e, 1), ((1,), (1,))) + log_col - base[:, :1]
        cnt = count[:, part]
        x = jnp.maximum(cnt, 1.0)
        cell = jnp.where(
            cnt > 0.0,
            (0.1 + 0.25 * (x * lax.rsqrt(x))) * (gap - jnp.log(x)),
            0.5 + 0.5 * jnp.tanh(0.5 * gap),
        )
        cell = split(cell)
        r_term = dot(left(cell, 1), right(e, 0), ((1,), (0,)))
        r_sum = r_term if r_sum is None else r_sum + r_term
        total = dot(wide, right(cell, 0), ((1,), (0,))).T.reshape(GROUP, SLICE, DIM)
        if adds_g:
            total += g_in[j * GROUP : (j + 1) * GROUP]
        g_out[j * GROUP : (j + 1) * GROUP] = total
    r_out[...] = r_sum + r_in[...] if adds_r else r_sum


def cells(which, table, prepared, pack, r_in=None, g_in=None):
    vmem = pl.BlockSpec(memory_space=pltpu.VMEM)
    counts, rows = prepared
    args = [counts[which], *rows, pack] + [a for a in (r_in, g_in) if a is not None]
    return pl.pallas_call(
        functools.partial(cells_kernel, which, r_in is not None, g_in is not None),
        in_specs=[pl.BlockSpec(memory_space=pltpu.SMEM)] + [vmem] * len(args),
        out_specs=[vmem] * 2,
        out_shape=[
            jax.ShapeDtypeStruct((2 * ROWS, DIM), jnp.float32),
            jax.ShapeDtypeStruct((8, SLICE, DIM), jnp.float32),
        ],
        compiler_params=pltpu.CompilerParams(vmem_limit_bytes=32 * 2**20),
        cost_estimate=pl.CostEstimate(
            flops=4 * 10**9, bytes_accessed=4 * 2**20, transcendentals=2**20
        ),
    )(table, *args)


def body(counts, row_marg, col_marg, log_total, row_embed, col_embed):
    core, xlo, xhi = (lax.axis_index(a) for a in ("core", "xlo", "xhi"))
    table = jnp.stack(
        [core, xhi, xlo]
        + [core, jnp.where(core == 0, xhi, 1 - xhi), 1 - xlo]
        + [core, jnp.where(core == 0, 1 - xhi, xhi), 1 - xlo]
        + [core, 1 - xhi, xlo]
    ).astype(jnp.int32)

    s_own = lax.all_to_all(pack_slice(col_embed, col_marg), "z", 0, 0)
    base_row = log_total[0] - jnp.log(row_marg.astype(jnp.float32))
    rb = jnp.concatenate([row_embed, jnp.broadcast_to(base_row[:, None], (ROWS, 128))], axis=1)
    by_slice = prepare_counts(table, (counts, fetch(counts, core_swap)))
    s_own, rb, rb_oth, by_slice = lax.optimization_barrier(
        (s_own, rb, fetch(rb, core_swap), by_slice)
    )
    prepared = (by_slice, prepare_rows(rb, rb_oth))

    s_a, s_b = fetch(s_own, side_a), fetch(s_own, side_b)
    r, g_own = cells(0, table, prepared, s_own)
    sent = fetch(g_own, side_b)
    s_far = fetch(s_a, side_b)
    r, g_a = cells(1, table, prepared, s_a, r)
    from_a = fetch(g_a, side_b)
    r, g_b = cells(2, table, prepared, s_b, r, sent)
    from_b = fetch(g_b, side_a)
    r, g = cells(3, table, prepared, s_far, r)
    g = lax.optimization_barrier(g + from_a) + from_b

    g = lax.all_to_all(g.reshape(64, 8, DIM), ("z", "y"), 0, 0)
    row_grad = (r[:ROWS] + fetch(r[ROWS:], core_swap)) * (1.0 / 64.0)
    g = jnp.sum(g, axis=0) * (1.0 / math.sqrt(131072.0))
    g = fetch(g, x_far)
    g = lax.all_to_all(jnp.broadcast_to(g[None], (32, 8, DIM)), ("core", "xlo", "y"), 0, 0)
    return row_grad, g.reshape(256, DIM)


def solution(mesh):
    fine = Mesh(mesh.devices.reshape(SIZES), AXES)
    both = ("xlo", "y", "core", "z", "xhi")
    col = ("z", "xhi")
    return jax.shard_map(
        body,
        mesh=fine,
        in_specs=(P(both, None), P(both), P(col), P(), P(both, None), P(col, None)),
        out_specs=(P(both, None), P(col, None)),
        check_vma=False,
    )
```

```python
import functools
import math

import jax
import jax.numpy as jnp
import numpy as np
from jax import lax
from jax.experimental import pallas as pl
from jax.experimental.pallas import tpu as pltpu
from jax.sharding import Mesh, PartitionSpec as P

AXES = ("xlo", "y", "core", "z", "xhi")
SIZES = (2, 8, 2, 8, 2)
DIM = 256
ROWS = 256
SLICE = 64
PACK = 72
STRIP = 64
GROUP = 4


def pairs_to(move):
    pairs = []
    for target in range(math.prod(SIZES)):
        at = dict(zip(AXES, (int(i) for i in np.unravel_index(target, SIZES))))
        at.update(move(at))
        pairs.append((int(np.ravel_multi_index([at[a] for a in AXES], SIZES)), target))
    return pairs


def core_swap(at):
    return {"core": 1 - at["core"]}


def x_pair(at):
    return {"xlo": 1 - at["xlo"]}


def x_next(at):
    return {"xlo": 1 - at["xlo"], "xhi": 1 - at["xhi"]}


def side_a(at):
    return x_next(at) if at["core"] else x_pair(at)


def side_b(at):
    return x_pair(at) if at["core"] else x_next(at)


def fetch(value, move):
    return lax.ppermute(value, AXES, pairs_to(move))


def split(value):
    high = value.astype(jnp.bfloat16)
    return high, (value - high.astype(jnp.float32)).astype(jnp.bfloat16)


def dot(a, b, dims):
    return lax.dot_general(
        a, b, dimension_numbers=(dims, ((), ())), preferred_element_type=jnp.float32
    )


def left(pair, axis):
    return jnp.concatenate([pair[0], pair[0], pair[1]], axis=axis)


def right(pair, axis):
    return jnp.concatenate([pair[0], pair[1], pair[0]], axis=axis)


def pack_kernel(embed, marg, out):
    start = (2 * lax.axis_index("core") + lax.axis_index("xlo")) * SLICE
    out[:, :SLICE, :] = jnp.broadcast_to(
        embed[pl.ds(pl.multiple_of(start, SLICE), SLICE), :][None], (8, SLICE, DIM)
    )
    logs = jnp.log(marg[...].astype(jnp.float32))
    out[:, SLICE:, :] = jnp.broadcast_to(logs[None], (8, PACK - SLICE, DIM))


def pack_slice(col_embed, col_marg):
    return pl.pallas_call(
        pack_kernel,
        out_shape=jax.ShapeDtypeStruct((8, PACK, DIM), jnp.float32),
        compiler_params=pltpu.CompilerParams(vmem_limit_bytes=60 * 2**20),
    )(col_embed, col_marg.reshape(1, DIM))


def rows_kernel(rb_own, rb_oth, rh, rl, th, tl, base):
    for k, rb in enumerate((rb_own, rb_oth)):
        part = slice(k * ROWS, (k + 1) * ROWS)
        value = rb[:, :DIM]
        rh[part, :], rl[part, :] = split(value)
        th[:, part], tl[:, part] = split(value.T)
        base[part, :] = rb[:, DIM:]


def prepare_rows(rb_own, rb_oth):
    tall = jax.ShapeDtypeStruct((2 * ROWS, DIM), jnp.bfloat16)
    wide = jax.ShapeDtypeStruct((DIM, 2 * ROWS), jnp.bfloat16)
    base = jax.ShapeDtypeStruct((2 * ROWS, 128), jnp.float32)
    vmem = pl.BlockSpec(memory_space=pltpu.VMEM)
    return pl.pallas_call(
        rows_kernel,
        in_specs=[vmem] * 2,
        out_specs=[vmem] * 5,
        out_shape=[tall, tall, wide, wide, base],
        compiler_params=pltpu.CompilerParams(vmem_limit_bytes=16 * 2**20),
        cost_estimate=pl.CostEstimate(flops=2**22, bytes_accessed=2**21, transcendentals=0),
    )(rb_own, rb_oth)


def counts_kernel(table, c_own, c_oth, *count_out):
    step = pl.program_id(0)
    steps = pl.num_programs(0)

    def work(counts):
        half = lax.broadcasted_iota(jnp.int32, (STRIP, 128), 1) < SLICE
        for which in range(4):
            core, xhi, xlo = (table[which * 3 + i] for i in range(3))
            near, far = xlo * SLICE, (1 - xlo) * SLICE
            for n in range(4):
                tiles = [
                    counts[:, pl.ds(pl.multiple_of((z * 4 + xhi * 2 + core) * 128, 128), 128)]
                    for z in (2 * n, 2 * n + 1)
                ]
                cnt = jnp.where(half, pltpu.roll(tiles[0], near, 1), pltpu.roll(tiles[1], far, 1))
                count_out[which][:, n * 128 : (n + 1) * 128] = cnt.astype(jnp.float32)

    @pl.when(step < steps // 2)
    def _():
        work(c_own)

    @pl.when(step >= steps // 2)
    def _():
        work(c_oth)


def prepare_counts(table, counts):
    half = ROWS // STRIP
    columns = counts[0].shape[1]
    return pl.pallas_call(
        counts_kernel,
        grid_spec=pltpu.PrefetchScalarGridSpec(
            num_scalar_prefetch=1,
            grid=(2 * half,),
            in_specs=[
                pl.BlockSpec((STRIP, columns), lambda i, w: (jnp.minimum(i, half - 1), 0)),
                pl.BlockSpec((STRIP, columns), lambda i, w: (jnp.maximum(i - half, 0), 0)),
            ],
            out_specs=[pl.BlockSpec((STRIP, 2 * DIM), lambda i, w: (i, 0))] * 4,
        ),
        out_shape=[jax.ShapeDtypeStruct((2 * ROWS, 2 * DIM), jnp.float32)] * 4,
        compiler_params=pltpu.CompilerParams(vmem_limit_bytes=54 * 2**20),
        cost_estimate=pl.CostEstimate(flops=2**22, bytes_accessed=2**21, transcendentals=0),
    )(table, *counts)


def cells_kernel(which, adds_r, adds_g, table, count, rh, rl, th, tl, base, pack, *rest):
    rest = list(rest)
    r_in = rest.pop(0) if adds_r else None
    g_in = rest.pop(0) if adds_g else None
    r_out, g_out = rest
    offset = (2 * table[3 * which] + table[3 * which + 2]) * SLICE
    near, far = lax.rem(DIM - offset, DIM), lax.rem(DIM + SLICE - offset, DIM)
    half = lax.broadcasted_iota(jnp.int32, (1, 128), 1) < SLICE
    tall, wide = left((rh[...], rl[...]), 1), left((th[...], tl[...]), 1)
    r_sum = None
    for j in range(8 // GROUP):
        part = slice(j * DIM, (j + 1) * DIM)
        here = pack[j * GROUP : (j + 1) * GROUP]
        e = split(here[:, :SLICE, :].reshape(DIM, DIM))
        logs = [here[i, SLICE : SLICE + 8, :] for i in range(GROUP)]
        log_col = jnp.concatenate(
            [
                jnp.where(
                    half,
                    pltpu.roll(logs[i], near, 1)[:1, :128],
                    pltpu.roll(logs[i + 1], far, 1)[:1, :128],
                )
                for i in (0, 2)
            ],
            axis=1,
        )
        gap = dot(tall, right(e, 1), ((1,), (1,))) + log_col - base[:, :1]
        cnt = count[:, part]
        x = jnp.maximum(cnt, 1.0)
        cell = jnp.where(
            cnt > 0.0,
            (0.1 + 0.25 * (x * lax.rsqrt(x))) * (gap - jnp.log(x)),
            0.5 + 0.5 * jnp.tanh(0.5 * gap),
        )
        cell = split(cell)
        r_term = dot(left(cell, 1), right(e, 0), ((1,), (0,)))
        r_sum = r_term if r_sum is None else r_sum + r_term
        total = dot(wide, right(cell, 0), ((1,), (0,))).T.reshape(GROUP, SLICE, DIM)
        if adds_g:
            total += g_in[j * GROUP : (j + 1) * GROUP]
        g_out[j * GROUP : (j + 1) * GROUP] = total
    r_out[...] = r_sum + r_in[...] if adds_r else r_sum


def cells(which, table, prepared, pack, r_in=None, g_in=None):
    vmem = pl.BlockSpec(memory_space=pltpu.VMEM)
    counts, rows = prepared
    args = [counts[which], *rows, pack] + [a for a in (r_in, g_in) if a is not None]
    return pl.pallas_call(
        functools.partial(cells_kernel, which, r_in is not None, g_in is not None),
        in_specs=[pl.BlockSpec(memory_space=pltpu.SMEM)] + [vmem] * len(args),
        out_specs=[vmem] * 2,
        out_shape=[
            jax.ShapeDtypeStruct((2 * ROWS, DIM), jnp.float32),
            jax.ShapeDtypeStruct((8, SLICE, DIM), jnp.float32),
        ],
        compiler_params=pltpu.CompilerParams(vmem_limit_bytes=32 * 2**20),
        cost_estimate=pl.CostEstimate(
            flops=4 * 10**9, bytes_accessed=4 * 2**20, transcendentals=2**20
        ),
    )(table, *args)


def body(counts, row_marg, col_marg, log_total, row_embed, col_embed):
    core, xlo, xhi = (lax.axis_index(a) for a in ("core", "xlo", "xhi"))
    table = jnp.stack(
        [core, xhi, xlo]
        + [core, jnp.where(core == 0, xhi, 1 - xhi), 1 - xlo]
        + [core, jnp.where(core == 0, 1 - xhi, xhi), 1 - xlo]
        + [core, 1 - xhi, xlo]
    ).astype(jnp.int32)

    s_own = lax.all_to_all(pack_slice(col_embed, col_marg), "z", 0, 0)
    base_row = log_total[0] - jnp.log(row_marg.astype(jnp.float32))
    rb = jnp.concatenate([row_embed, jnp.broadcast_to(base_row[:, None], (ROWS, 128))], axis=1)
    by_slice = prepare_counts(table, (counts, fetch(counts, core_swap)))
    s_own, rb, rb_oth, by_slice = lax.optimization_barrier(
        (s_own, rb, fetch(rb, core_swap), by_slice)
    )
    prepared = (by_slice, prepare_rows(rb, rb_oth))

    s_a, s_b = fetch(s_own, side_a), fetch(s_own, side_b)
    r, g_own = cells(0, table, prepared, s_own)
    sent = fetch(g_own, side_b)
    s_far = fetch(s_a, side_b)
    r, g_a = cells(1, table, prepared, s_a, r)
    from_a = fetch(g_a, side_b)
    r, g_b = cells(2, table, prepared, s_b, r, sent)
    from_b = fetch(g_b, side_a)
    r, g = cells(3, table, prepared, s_far, r)
    g = lax.optimization_barrier(g + from_a) + from_b

    g = lax.all_to_all(g.reshape(64, 8, DIM), ("z", "y"), 0, 0)
    row_grad = (r[:ROWS] + fetch(r[ROWS:], core_swap)) * (1.0 / 64.0)
    g = jnp.sum(g, axis=0) * (1.0 / math.sqrt(131072.0))
    g = fetch(g, x_next)
    g = lax.all_to_all(jnp.broadcast_to(g[None], (32, 8, DIM)), ("core", "xlo", "y"), 0, 0)
    g = g.reshape(2, 2, SLICE, DIM)
    col_grad = jnp.stack([g[:, 1], g[:, 0]], axis=1)
    return row_grad, col_grad.reshape(256, DIM)


def solution(mesh):
    fine = Mesh(mesh.devices.reshape(SIZES), AXES)
    both = ("xlo", "y", "core", "z", "xhi")
    col = ("z", "xhi")
    return jax.shard_map(
        body,
        mesh=fine,
        in_specs=(P(both, None), P(both), P(col), P(), P(both, None), P(col, None)),
        out_specs=(P(both, None), P(col, None)),
        check_vma=False,
    )
```
